128 devices in a mesh: cuts: 8 (over z, x_lo), space: 16 (over y, x_hi, core).
Axes of the slice: x: 4 (x_hi: 2, x_lo: 2; x = x_hi * 2 + x_lo), y: 4, z: 4, core: 2. Of those that a mesh axis runs over, the one named last changes fastest.
Arguments:
- states: float32 [8, 512, 2048], P('cuts', 'space'), may hold values from -6 to 6
- stream: float32 [512, 2048], P('space'), may hold values from -4 to 4
Outputs:
- new_states: float32 [8, 512, 2048], P('cuts', 'space')
The draws below stay inside these ranges and needn't reach their ends.
All inputs are finite; a program needn't handle non-finite values.
Results may differ from the reference program's by a relative error of at most 0.00002.
Values sent between devices are 32-bit elements; how exact they have to be, the bound alone decides.
A program may use at most 64 MiB of HBM per device.

```python
import jax
import jax.numpy as jnp
from jax import lax

COLS = 2048
FINE_STEPS = 4
SLICES = 8
NY = 512


def block_scale(own_key, shape, cuts, low, largest):
    loudness = 1.0
    for axis_at, shards_of in cuts:
        steps = jax.random.uniform(jax.random.fold_in(jax.random.fold_in(own_key, 6), axis_at), (shards_of,), jnp.float32, low / len(cuts), largest / len(cuts))
        loudness = loudness * jnp.repeat(jnp.exp(steps), shape[axis_at] // shards_of).reshape((-1,) + (1,) * (len(shape) - 1 - axis_at))
    return loudness


def bell_draw(key, shape, deviation, reach, split=(), dtype=jnp.bfloat16):
    array = deviation * jax.random.normal(key, shape, jnp.float32)
    if split:
        array = array * block_scale(key, shape, split, -0.22, 0.18)
    return jnp.clip(array, -reach, reach).astype(dtype)


def setup_inputs(seed: int = 0) -> dict:
    seeds = jax.random.split(jax.random.key(seed), 3)
    return {
        "states": bell_draw(seeds[0], (SLICES, NY, COLS), 1.0, 6.0, ((0, 8), (1, 16)), jnp.float32),
        "stream": bell_draw(seeds[1], (NY, COLS), 1.0, 4.0, ((0, 16),), jnp.float32),
    }


VISCOSITY = 0.2
FINE_DT = 0.25


def wrap_rows(field):
    return jnp.concatenate([field[-1:], field, field[:1]], axis=0)


def velocity(padded, spacing):
    middle = padded[1:-1]
    speed_x = (padded[2:] - padded[:-2]) / (2.0 * spacing)
    speed_y = -((jnp.roll(middle, -1, 1) - jnp.roll(middle, 1, 1)) / (2.0 * spacing))
    return speed_x, speed_y


def tendency(padded, speed_x, speed_y, spacing):
    middle = padded[1:-1]
    right_col = jnp.roll(middle, -1, 1)
    left_col = jnp.roll(middle, 1, 1)
    upper_row = padded[2:]
    lower_row = padded[:-2]
    slope_x = (right_col - left_col) / (2.0 * spacing)
    slope_y = (upper_row - lower_row) / (2.0 * spacing)
    laplace = (upper_row + lower_row + right_col + left_col - 4.0 * middle) / (spacing * spacing)
    return -speed_x * slope_x - speed_y * slope_y + VISCOSITY * laplace


def runge_step(field, speed_x, speed_y, spacing, step_size, pad_fn):
    segment_one = tendency(pad_fn(field), speed_x, speed_y, spacing)
    segment_two = tendency(pad_fn(field + (0.5 * step_size) * segment_one), speed_x, speed_y, spacing)
    segment_three = tendency(pad_fn(field + (0.5 * step_size) * segment_two), speed_x, speed_y, spacing)
    segment_four = tendency(pad_fn(field + step_size * segment_three), speed_x, speed_y, spacing)
    return field + (step_size / 6.0) * (segment_one + 2.0 * segment_two + 2.0 * segment_three + segment_four)


def restrict(field):
    leading = field.shape[:-2]
    height, width = field.shape[-2:]
    return field.reshape(leading + (height // 4, 4, width // 4, 4)).mean(axis=(-3, -1))


def prolong(field):
    return jnp.repeat(jnp.repeat(field, 4, axis=-2), 4, axis=-1)


def reference(states, stream):
    fine_u, fine_v = velocity(wrap_rows(stream), 1.0)
    coarse_u, coarse_v = velocity(wrap_rows(restrict(stream)), 4.0)

    def fine_prop(field):
        for _ in range(FINE_STEPS):
            field = runge_step(field, fine_u, fine_v, 1.0, FINE_DT, wrap_rows)
        return field

    def coarse_prop(field):
        return runge_step(field, coarse_u, coarse_v, 4.0, FINE_DT * FINE_STEPS, wrap_rows)

    fine_end = lax.map(fine_prop, states)
    coarse_old = lax.map(lambda field: coarse_prop(restrict(field)), states)
    coarse_gap = restrict(fine_end) - coarse_old
    current = restrict(states[0])
    stepped_all = []
    for member in range(states.shape[0]):
        stepped = coarse_prop(current)
        stepped_all.append(stepped)
        current = stepped + coarse_gap[member]
    return fine_end + prolong(jnp.stack(stepped_all) - coarse_old)
```

```python
import jax
import jax.numpy as jnp
from jax import lax
from jax.experimental import pallas as pl
from jax.experimental.pallas import tpu as pltpu
from jax.sharding import PartitionSpec as P

MESH = pl.DeviceIdType.MESH
LANES = 128
COLS = 2048
FT = COLS // LANES
CT = FT // 4
BAND = 32
HALO = 16
WIDE = BAND + 2 * HALO
SLICES = 8
SPACE = 16
REACH = 4
CROWS = 8
CWIDE = CROWS * (2 * REACH + 1)
FINE_STEPS = 4
F32 = jnp.float32


def scales(step, kappa):
    gains = [step / (4 - s) / kappa for s in range(4)]
    betas = [1.0] * 4
    for s in (2, 1, 0):
        betas[s] = betas[s + 1] * gains[s + 1]
    return betas, betas[0] * gains[0]


FINE_BETAS, FINE_START = scales(0.25, 1.25)
COARSE_BETAS, COARSE_START = scales(1.0, 20.0)


def rows_up(t):
    return jnp.concatenate([t[1:], pltpu.roll(t[:1], 7, 1)], axis=0)


def rows_down(t):
    return jnp.concatenate([pltpu.roll(t[-1:], 1, 1), t[:-1]], axis=0)


def columns(left, t, right):
    lane = lax.broadcasted_iota(jnp.int32, t.shape, 2)
    west = jnp.where(lane == 0, pltpu.roll(left, 1, 2), pltpu.roll(t, 1, 2))
    east = jnp.where(lane == LANES - 1, pltpu.roll(right, LANES - 1, 2), pltpu.roll(t, LANES - 1, 2))
    return east, west


def coefficients(psi, east, west):
    ce = 0.25 - 0.3125 * (rows_up(psi) - rows_down(psi))
    cn = 0.25 + 0.3125 * (east - west)
    return ce, cn


def operator(t, east, west, ce, cw, cn, cs):
    return ce * east + cw * west + cn * rows_up(t) + cs * rows_down(t) - t


def matmul(x, m):
    return jnp.dot(x, m, precision=lax.Precision.HIGHEST, preferred_element_type=F32)


def kernel(
    states, stream, out,
    xwin, swin, base, ta, tb, fce, fcw, fcn, fcs, shrink, grow, rows, cbuf, wstream, wgap, spw, pay, nbuf, newc,
    local_sem, halo_send, halo_recv, sc_send, sc_recv, a_send, a_recv, b_send, b_recv, c_send, c_recv,
):
    n = lax.axis_index("cuts")
    b = lax.axis_index("space")

    def at_space(j):
        return (n, lax.rem(b + (SPACE + j), SPACE))

    offsets = [j for d in range(1, REACH + 1) for j in (-d, d)]

    own_x = pltpu.make_async_copy(states, xwin.at[pl.ds(HALO // 8, BAND // 8)], local_sem.at[0])
    own_s = pltpu.make_async_copy(stream, swin.at[pl.ds(HALO // 8, BAND // 8)], local_sem.at[1])
    xrows = xwin.reshape(WIDE * FT, LANES)
    srows = swin.reshape(WIDE * FT, LANES)
    own_s.start()
    own_x.start()

    pay[...] = jnp.zeros_like(pay)
    newc[...] = jnp.zeros_like(newc)

    barrier = pltpu.get_barrier_semaphore()
    for j in offsets:
        pl.semaphore_signal(barrier, inc=1, device_id=at_space(j), device_id_type=MESH)
    for k in range(1, SLICES):
        pl.semaphore_signal(
            barrier, inc=1, device_id=(lax.rem(n + k, SLICES), b), device_id_type=MESH
        )
    pl.semaphore_wait(barrier, len(offsets) + SLICES - 1)

    halos = []
    for at, (source, window) in enumerate(((stream, swin), (states, xwin))):
        for side, (j, first, target) in enumerate(((1, BAND - HALO, 0), (-1, 0, HALO + BAND))):
            halos.append(
                pltpu.make_async_remote_copy(
                    src_ref=source.at[pl.ds(first // 8, HALO // 8)],
                    dst_ref=window.at[pl.ds(target // 8, HALO // 8)],
                    send_sem=halo_send.at[2 * at + side],
                    recv_sem=halo_recv.at[2 * at + side],
                    device_id=at_space(j),
                    device_id_type=MESH,
                )
            )
            halos[-1].start()

    fine_at = lax.broadcasted_iota(jnp.int32, (4 * LANES, LANES), 0)
    coarse_at = lax.broadcasted_iota(jnp.int32, (4 * LANES, LANES), 1)
    shrink[...] = jnp.where((fine_at >> 2) == coarse_at, 0.0625, 0.0).astype(F32)
    fine_at = lax.broadcasted_iota(jnp.int32, (LANES, 4 * LANES), 1)
    coarse_at = lax.broadcasted_iota(jnp.int32, (LANES, 4 * LANES), 0)
    grow[...] = jnp.where((fine_at >> 2) == coarse_at, 1.0, 0.0).astype(F32)

    def windows(tiles, target):
        lane = lax.broadcasted_iota(jnp.int32, (CROWS, LANES), 1)
        right = [pltpu.roll(t, 32, 1) for t in tiles]
        left = [pltpu.roll(t, LANES - 32, 1) for t in tiles]
        for j in range(CT):
            target[2 * j] = jnp.where(lane < 32, right[(j - 1) % CT], right[j])
            target[2 * j + 1] = jnp.where(lane < LANES - 32, left[j], left[(j + 1) % CT])

    own_s.wait()
    for c in range(CT):
        for m in range(4):
            for half in range(2):
                parts = [srows[pl.ds(2 * FT * 8 + (4 * c + m) * 8 + 4 * half + i, 4, stride=FT * 8)] for i in range(4)]
                rows[pl.ds(8 * c + 4 * half, 4), pl.ds(m * LANES, LANES)] = parts[0] + parts[1] + parts[2] + parts[3]
    small = matmul(rows[pl.ds(0, CROWS * CT)], shrink[...])
    for c in range(CT):
        for half in range(2):
            cbuf[c, pl.ds(half, 4, stride=2)] = small[8 * c + 4 * half:8 * c + 4 * half + 4]
    windows([cbuf[c, pl.ds(0, CROWS)] for c in range(CT)], wstream)
    spreads = []
    for at, j in enumerate(offsets):
        spreads.append(
            pltpu.make_async_remote_copy(
                src_ref=wstream.at[n],
                dst_ref=spw.at[pl.ds(CROWS * (REACH - j), CROWS)],
                send_sem=sc_send.at[at],
                recv_sem=sc_recv.at[at],
                device_id=at_space(j),
                device_id_type=MESH,
            )
        )
        spreads[-1].start()
    spw[pl.ds(CROWS * REACH, CROWS)] = wstream[n]
    own_x.wait()

    for halo in halos[:2]:
        halo.wait_recv()

    def window_tile(window, c):
        return jnp.stack(
            [window[pl.ds(c * 8 + r, 8, stride=FT * 8)] for r in range(8)]
        )

    def weights(c, carry):
        psi = window_tile(srows, c)
        east, west = columns(
            window_tile(srows, lax.rem(c + FT - 1, FT)), psi, window_tile(srows, lax.rem(c + 1, FT))
        )
        ce, cn = coefficients(psi, east, west)
        fce[c] = ce
        fcw[c] = 0.5 - ce
        fcn[c] = cn
        fcs[c] = 0.5 - cn
        return carry

    lax.fori_loop(0, FT, weights, 0)

    for halo in halos[2:]:
        halo.wait_recv()

    def begin(c, carry):
        base[c] = window_tile(xrows, c)
        return carry

    lax.fori_loop(0, FT, begin, 0)

    def restrict(tile):
        for c in range(CT):
            for m in range(4):
                t = tile(4 * c + m)
                for q in range(2):
                    rows[pl.ds(8 * (2 * c + q), 8), pl.ds(m * LANES, LANES)] = (
                        t[4 * q] + t[4 * q + 1] + t[4 * q + 2] + t[4 * q + 3]
                    )
        small = matmul(rows[...], shrink[...])
        return [
            jnp.stack([small[8 * (2 * c + q):8 * (2 * c + q + 1)] for q in range(2)]) for c in range(CT)
        ]

    cpsi = restrict(lambda c: window_tile(srows, c))
    cweights = []
    for c in range(CT):
        east, west = columns(cpsi[c - 1], cpsi[c], cpsi[(c + 1) % CT])
        ce, cn = coefficients(cpsi[c], east, west)
        cweights.append((ce, 0.5 - ce, cn, 0.5 - cn))
    start = restrict(lambda c: base[c])
    old = start
    for s in range(4):
        moved = []
        for c in range(CT):
            east, west = columns(old[c - 1], old[c], old[(c + 1) % CT])
            change = operator(old[c], east, west, *cweights[c])
            if s == 0:
                change = COARSE_START * change
            moved.append(COARSE_BETAS[s] * start[c] + change)
        old = moved

    def fine_stage(s, src, dst):
        def tile(c, carry):
            t = src[c]
            east, west = columns(src[lax.rem(c + FT - 1, FT)], t, src[lax.rem(c + 1, FT)])
            change = operator(t, east, west, fce[c], fcw[c], fcn[c], fcs[c])
            if s == 0:
                change = FINE_START * change
            dst[c] = FINE_BETAS[s] * base[c] + change
            return carry

        lax.fori_loop(0, FT, tile, 0)

    def fine_step(step, carry):
        fine_stage(0, base, ta)
        fine_stage(1, ta, tb)
        fine_stage(2, tb, ta)
        fine_stage(3, ta, base)
        return carry

    lax.fori_loop(0, FINE_STEPS, fine_step, 0)

    ended = restrict(lambda c: base[c])
    gap = [ended[c] - old[c] for c in range(CT)]
    gap = [jnp.where(n == 0, old[c] + gap[c], gap[c]) for c in range(CT)]
    for c in range(CT):
        for q in range(2):
            cbuf[c, pl.ds(4 + q, 8, stride=2)] = gap[c][q]
    windows([cbuf[c, pl.ds(8, CROWS)] for c in range(CT)], wgap)

    middle = pl.ds(CROWS * REACH, CROWS)

    def gap_copy(k, m):
        return pltpu.make_async_remote_copy(
            src_ref=wgap.at[k],
            dst_ref=pay.at[m, middle],
            send_sem=a_send.at[k],
            recv_sem=a_recv.at[m],
            device_id=(k, b),
            device_id_type=MESH,
        )

    for k in range(SLICES):
        @pl.when((n != k) & (n < SLICES - 1))
        def _():
            gap_copy(k, n).start()

    @pl.when(n < SLICES - 1)
    def _():
        pay[n, middle] = wgap[n]

    for spread in spreads:
        spread.wait()
    psi = jnp.stack([spw[pl.ds(4 + r, 8, stride=8)] for r in range(8)])
    ce, cn = coefficients(psi, pltpu.roll(psi, LANES - 1, 2), pltpu.roll(psi, 1, 2))
    chain_weights = (ce, 0.5 - ce, cn, 0.5 - cn)

    for m in range(SLICES - 1):
        @pl.when(n != m)
        def _():
            gap_copy(m, m).wait_recv()

    gathers = []
    for at, j in enumerate(offsets):
        count = SLICES + 1 - 2 * abs(j)
        gathers.append(
            pltpu.make_async_remote_copy(
                src_ref=pay.at[pl.ds(0, count), middle],
                dst_ref=pay.at[pl.ds(0, count), pl.ds(CROWS * (REACH - j), CROWS)],
                send_sem=b_send.at[at],
                recv_sem=b_recv.at[at],
                device_id=at_space(j),
                device_id_type=MESH,
            )
        )
        gathers[-1].start()
    for gather in gathers:
        gather.wait_recv()

    def new_copy(i, k):
        return pltpu.make_async_remote_copy(
            src_ref=nbuf.at[i, middle],
            dst_ref=newc.at[k],
            send_sem=c_send.at[i],
            recv_sem=c_recv.at[k],
            device_id=(i, b),
            device_id_type=MESH,
        )

    def link(i, current):
        t = current
        for s in range(4):
            change = operator(t, pltpu.roll(t, LANES - 1, 2), pltpu.roll(t, 1, 2), *chain_weights)
            if s == 0:
                change = COARSE_START * change
            t = COARSE_BETAS[s] * current + change
        for r in range(8):
            nbuf[i, pl.ds(4 + r, 8, stride=8)] = t[r]

        @pl.when(i != n)
        def _():
            new_copy(i, n).start()

        @pl.when(i == n)
        def _():
            newc[n] = nbuf[i, middle]

        late = lax.rem(i, SLICES - 1)
        return t + jnp.stack([pay[late, pl.ds(4 + r, 8, stride=8)] for r in range(8)])

    first = jnp.stack([pay[0, pl.ds(4 + r, 8, stride=8)] for r in range(8)])
    lax.fori_loop(1, SLICES, link, first)

    for k in range(SLICES):
        @pl.when((n != k) & (n > 0))
        def _():
            new_copy(k, k).wait_recv()

    lane = lax.broadcasted_iota(jnp.int32, (CROWS, LANES), 1)
    for c in range(CT):
        cbuf[c, pl.ds(8, CROWS)] = jnp.where(
            lane < LANES // 2, pltpu.roll(newc[2 * c], LANES - 32, 1), pltpu.roll(newc[2 * c + 1], 32, 1)
        )
    parts = []
    for c in range(CT):
        for q in range(2):
            new = cbuf[c, pl.ds(4 + q, 8, stride=2)]
            new = jnp.where(n == 0, old[c][q], new)
            parts.append(new - old[c][q])
    rows[...] = matmul(jnp.concatenate(parts, axis=0), grow[...])
    for c in range(CT):
        for m in range(4):
            t = base[4 * c + m]
            for r in range(8):
                xrows[pl.ds((4 * c + m) * 8 + r, 8, stride=FT * 8)] = (
                    t[r] + rows[pl.ds(8 * (2 * c + r // 4), 8), pl.ds(m * LANES, LANES)]
                )
    result = pltpu.make_async_copy(xwin.at[pl.ds(HALO // 8, BAND // 8)], out, local_sem.at[0])
    result.start()

    for halo in halos:
        halo.wait_send()
    for k in range(SLICES):
        @pl.when((n != k) & (n < SLICES - 1))
        def _():
            gap_copy(k, n).wait_send()
    for gather in gathers:
        gather.wait_send()
    for i in range(1, SLICES):
        @pl.when(n != i)
        def _():
            new_copy(i, n).wait_send()
    result.wait()


def per_device(states, stream):
    tiles = pltpu.VMEM((FT, 8, 8, LANES), F32)

    def tiled(x):
        return x.reshape(BAND // 8, 8, FT, LANES).transpose(0, 2, 1, 3)

    ended = pl.pallas_call(
        kernel,
        out_shape=jax.ShapeDtypeStruct((BAND // 8, FT, 8, LANES), F32),
        in_specs=[pl.BlockSpec(memory_space=pl.ANY)] * 2,
        out_specs=pl.BlockSpec(memory_space=pl.ANY),
        scratch_shapes=[
            pltpu.VMEM((WIDE // 8, FT, 8, LANES), F32),
            pltpu.VMEM((WIDE // 8, FT, 8, LANES), F32),
            tiles, tiles, tiles, tiles, tiles, tiles, tiles,
            pltpu.VMEM((4 * LANES, LANES), F32),
            pltpu.VMEM((LANES, 4 * LANES), F32),
            pltpu.VMEM((2 * CT * 8, 4 * LANES), F32),
            pltpu.VMEM((CT, 24, LANES), F32),
            pltpu.VMEM((SLICES, CROWS, LANES), F32),
            pltpu.VMEM((SLICES, CROWS, LANES), F32),
            pltpu.VMEM((CWIDE, LANES), F32),
            pltpu.VMEM((SLICES - 1, CWIDE, LANES), F32),
            pltpu.VMEM((SLICES, CWIDE, LANES), F32),
            pltpu.VMEM((SLICES, CROWS, LANES), F32),
            pltpu.SemaphoreType.DMA((2,)),
            pltpu.SemaphoreType.DMA((4,)),
            pltpu.SemaphoreType.DMA((4,)),
            pltpu.SemaphoreType.DMA((2 * REACH,)),
            pltpu.SemaphoreType.DMA((2 * REACH,)),
            pltpu.SemaphoreType.DMA((SLICES,)),
            pltpu.SemaphoreType.DMA((SLICES,)),
            pltpu.SemaphoreType.DMA((2 * REACH,)),
            pltpu.SemaphoreType.DMA((2 * REACH,)),
            pltpu.SemaphoreType.DMA((SLICES,)),
            pltpu.SemaphoreType.DMA((SLICES,)),
        ],
        compiler_params=pltpu.CompilerParams(
            collective_id=0, has_side_effects=True, vmem_limit_bytes=32 * 1024 * 1024
        ),
    )(tiled(states), tiled(stream))
    return ended.transpose(0, 2, 1, 3).reshape(1, BAND, COLS)


def solution(mesh):
    in_specs = (P("cuts", "space", None), P("space", None))
    out_specs = P("cuts", "space", None)
    return jax.shard_map(
        per_device, mesh=mesh, in_specs=in_specs, out_specs=out_specs, check_vma=False
    )
```

```python
import jax
import jax.numpy as jnp
from jax import lax
from jax.experimental import pallas as pl
from jax.experimental.pallas import tpu as pltpu
from jax.sharding import PartitionSpec as P

MESH = pl.DeviceIdType.MESH
LANES = 128
COLS = 2048
FT = COLS // LANES
CT = FT // 4
BAND = 32
HALO = 16
WIDE = BAND + 2 * HALO
SLICES = 8
SPACE = 16
REACH = 4
CROWS = 8
CWIDE = CROWS * (2 * REACH + 1)
FINE_STEPS = 4
F32 = jnp.float32


def scales(step, kappa):
    gains = [step / (4 - s) / kappa for s in range(4)]
    betas = [1.0] * 4
    for s in (2, 1, 0):
        betas[s] = betas[s + 1] * gains[s + 1]
    return betas, betas[0] * gains[0]


FINE_BETAS, FINE_START = scales(0.25, 1.25)
COARSE_BETAS, COARSE_START = scales(1.0, 20.0)


def rows_up(t):
    return jnp.concatenate([t[1:], pltpu.roll(t[:1], 7, 1)], axis=0)


def rows_down(t):
    return jnp.concatenate([pltpu.roll(t[-1:], 1, 1), t[:-1]], axis=0)


def columns(left, t, right):
    lane = lax.broadcasted_iota(jnp.int32, t.shape, 2)
    west = jnp.where(lane == 0, pltpu.roll(left, 1, 2), pltpu.roll(t, 1, 2))
    east = jnp.where(lane == LANES - 1, pltpu.roll(right, LANES - 1, 2), pltpu.roll(t, LANES - 1, 2))
    return east, west


def coefficients(psi, east, west):
    ce = 0.25 - 0.3125 * (rows_up(psi) - rows_down(psi))
    cn = 0.25 + 0.3125 * (east - west)
    return ce, cn


def operator(t, east, west, ce, cw, cn, cs):
    return ce * east + cw * west + cn * rows_up(t) + cs * rows_down(t) - t


def matmul(x, m):
    return jnp.dot(x, m, precision=lax.Precision.HIGHEST, preferred_element_type=F32)


def kernel(
    states, stream, out,
    xwin, swin, base, ta, tb, fce, fcw, fcn, fcs, shrink, grow, rows, cbuf, wstream, wgap, spw, pay, nbuf, newc,
    local_sem, halo_send, halo_recv, sc_send, sc_recv, a_send, a_recv, b_send, b_recv, c_send, c_recv,
):
    n = lax.axis_index("cuts")
    b = lax.axis_index("space")

    def at_space(j):
        return (n, lax.rem(b + (SPACE + j), SPACE))

    offsets = [j for d in range(1, REACH + 1) for j in (-d, d)]

    own_x = pltpu.make_async_copy(states, xwin.at[pl.ds(HALO // 8, BAND // 8)], local_sem.at[0])
    own_s = pltpu.make_async_copy(stream, swin.at[pl.ds(HALO // 8, BAND // 8)], local_sem.at[1])
    xrows = xwin.reshape(WIDE * FT, LANES)
    srows = swin.reshape(WIDE * FT, LANES)
    own_s.start()
    own_x.start()

    pay[...] = jnp.zeros_like(pay)
    newc[...] = jnp.zeros_like(newc)

    barrier = pltpu.get_barrier_semaphore()
    for j in offsets:
        pl.semaphore_signal(barrier, inc=1, device_id=at_space(j), device_id_type=MESH)
    for k in range(1, SLICES):
        pl.semaphore_signal(
            barrier, inc=1, device_id=(lax.rem(n + k, SLICES), b), device_id_type=MESH
        )
    pl.semaphore_wait(barrier, len(offsets) + SLICES - 1)

    halos = []
    for at, (source, window) in enumerate(((stream, swin), (states, xwin))):
        for side, (j, first, target) in enumerate(((1, BAND - HALO, 0), (-1, 0, HALO + BAND))):
            halos.append(
                pltpu.make_async_remote_copy(
                    src_ref=source.at[pl.ds(first // 8, HALO // 8)],
                    dst_ref=window.at[pl.ds(target // 8, HALO // 8)],
                    send_sem=halo_send.at[2 * at + side],
                    recv_sem=halo_recv.at[2 * at + side],
                    device_id=at_space(j),
                    device_id_type=MESH,
                )
            )
            halos[-1].start()

    fine_at = lax.broadcasted_iota(jnp.int32, (4 * LANES, LANES), 0)
    coarse_at = lax.broadcasted_iota(jnp.int32, (4 * LANES, LANES), 1)
    shrink[...] = jnp.where((fine_at >> 2) == coarse_at, 0.0625, 0.0).astype(F32)
    fine_at = lax.broadcasted_iota(jnp.int32, (LANES, 4 * LANES), 1)
    coarse_at = lax.broadcasted_iota(jnp.int32, (LANES, 4 * LANES), 0)
    grow[...] = jnp.where((fine_at >> 2) == coarse_at, 1.0, 0.0).astype(F32)

    def windows(tiles, target):
        lane = lax.broadcasted_iota(jnp.int32, (CROWS, LANES), 1)
        right = [pltpu.roll(t, 32, 1) for t in tiles]
        left = [pltpu.roll(t, LANES - 32, 1) for t in tiles]
        for j in range(CT):
            target[2 * j] = jnp.where(lane < 32, right[(j - 1) % CT], right[j])
            target[2 * j + 1] = jnp.where(lane < LANES - 32, left[j], left[(j + 1) % CT])

    own_s.wait()
    for c in range(CT):
        for m in range(4):
            for half in range(2):
                parts = [srows[pl.ds(2 * FT * 8 + (4 * c + m) * 8 + 4 * half + i, 4, stride=FT * 8)] for i in range(4)]
                rows[pl.ds(8 * c + 4 * half, 4), pl.ds(m * LANES, LANES)] = parts[0] + parts[1] + parts[2] + parts[3]
    small = matmul(rows[pl.ds(0, CROWS * CT)], shrink[...])
    for c in range(CT):
        for half in range(2):
            cbuf[c, pl.ds(half, 4, stride=2)] = small[8 * c + 4 * half:8 * c + 4 * half + 4]
    windows([cbuf[c, pl.ds(0, CROWS)] for c in range(CT)], wstream)
    spreads = []
    for at, j in enumerate(offsets):
        spreads.append(
            pltpu.make_async_remote_copy(
                src_ref=wstream.at[n],
                dst_ref=spw.at[pl.ds(CROWS * (REACH - j), CROWS)],
                send_sem=sc_send.at[at],
                recv_sem=sc_recv.at[at],
                device_id=at_space(j),
                device_id_type=MESH,
            )
        )
        spreads[-1].start()
    spw[pl.ds(CROWS * REACH, CROWS)] = wstream[n]
    own_x.wait()

    for halo in halos[:2]:
        halo.wait_recv()

    def window_tile(window, c):
        return jnp.stack(
            [window[pl.ds(c * 8 + r, 8, stride=FT * 8)] for r in range(8)]
        )

    def weights(c, carry):
        psi = window_tile(srows, c)
        east, west = columns(
            window_tile(srows, lax.rem(c + FT - 1, FT)), psi, window_tile(srows, lax.rem(c + 1, FT))
        )
        ce, cn = coefficients(psi, east, west)
        fce[c] = ce
        fcw[c] = 0.5 - ce
        fcn[c] = cn
        fcs[c] = 0.5 - cn
        return carry

    lax.fori_loop(0, FT, weights, 0)

    for halo in halos[2:]:
        halo.wait_recv()

    def begin(c, carry):
        base[c] = window_tile(xrows, c)
        return carry

    lax.fori_loop(0, FT, begin, 0)

    def restrict(tile):
        for c in range(CT):
            for m in range(4):
                t = tile(4 * c + m)
                for q in range(2):
                    rows[pl.ds(8 * (2 * c + q), 8), pl.ds(m * LANES, LANES)] = (
                        t[4 * q] + t[4 * q + 1] + t[4 * q + 2] + t[4 * q + 3]
                    )
        small = matmul(rows[...], shrink[...])
        return [
            jnp.stack([small[8 * (2 * c + q):8 * (2 * c + q + 1)] for q in range(2)]) for c in range(CT)
        ]

    cpsi = restrict(lambda c: window_tile(srows, c))
    cweights = []
    for c in range(CT):
        east, west = columns(cpsi[c - 1], cpsi[c], cpsi[(c + 1) % CT])
        ce, cn = coefficients(cpsi[c], east, west)
        cweights.append((ce, 0.5 - ce, cn, 0.5 - cn))
    start = restrict(lambda c: base[c])
    old = start
    for s in range(4):
        moved = []
        for c in range(CT):
            east, west = columns(old[c - 1], old[c], old[(c + 1) % CT])
            change = operator(old[c], east, west, *cweights[c])
            if s == 0:
                change = COARSE_START * change
            moved.append(COARSE_BETAS[s] * start[c] + change)
        old = moved

    def fine_stage(s, src, dst):
        lane = lax.broadcasted_iota(jnp.int32, (4, 8, LANES), 2)

        def west_of(t):
            return pltpu.roll(t, 1, 2)

        def east_of(t):
            return pltpu.roll(t, LANES - 1, 2)

        for first in (0, 4):
            part = pl.ds(first, 4)
            west_before = west_of(src[FT - 1, part])
            t = src[0, part]
            east_now = east_of(t)
            for c in range(FT):
                after = src[(c + 1) % FT, part]
                west_now, east_after = west_of(t), east_of(after)
                west = jnp.where(lane == 0, west_before, west_now)
                east = jnp.where(lane == LANES - 1, east_after, east_now)
                if first == 0:
                    up = jnp.concatenate([t[1:], src[c, pl.ds(4, 1)]], axis=0)
                    down = jnp.concatenate([pltpu.roll(src[c, pl.ds(7, 1)], 1, 1), t[:-1]], axis=0)
                else:
                    up = jnp.concatenate([t[1:], pltpu.roll(src[c, pl.ds(0, 1)], 7, 1)], axis=0)
                    down = jnp.concatenate([src[c, pl.ds(3, 1)], t[:-1]], axis=0)
                change = (
                    fce[c, part] * east + fcw[c, part] * west + fcn[c, part] * up + fcs[c, part] * down - t
                )
                if s == 0:
                    change = FINE_START * change
                dst[c, part] = FINE_BETAS[s] * base[c, part] + change
                t, west_before, east_now = after, west_now, east_after

    def fine_step(step, carry):
        fine_stage(0, base, ta)
        fine_stage(1, ta, tb)
        fine_stage(2, tb, ta)
        fine_stage(3, ta, base)
        return carry

    lax.fori_loop(0, FINE_STEPS, fine_step, 0)

    ended = restrict(lambda c: base[c])
    gap = [ended[c] - old[c] for c in range(CT)]
    gap = [jnp.where(n == 0, old[c] + gap[c], gap[c]) for c in range(CT)]
    for c in range(CT):
        for q in range(2):
            cbuf[c, pl.ds(4 + q, 8, stride=2)] = gap[c][q]
    windows([cbuf[c, pl.ds(8, CROWS)] for c in range(CT)], wgap)

    middle = pl.ds(CROWS * REACH, CROWS)

    def gap_copy(k, m):
        return pltpu.make_async_remote_copy(
            src_ref=wgap.at[k],
            dst_ref=pay.at[m, middle],
            send_sem=a_send.at[k],
            recv_sem=a_recv.at[m],
            device_id=(k, b),
            device_id_type=MESH,
        )

    for k in range(SLICES):
        @pl.when((n != k) & (n < SLICES - 1))
        def _():
            gap_copy(k, n).start()

    @pl.when(n < SLICES - 1)
    def _():
        pay[n, middle] = wgap[n]

    for spread in spreads:
        spread.wait()
    psi = jnp.stack([spw[pl.ds(4 + r, 8, stride=8)] for r in range(8)])
    ce, cn = coefficients(psi, pltpu.roll(psi, LANES - 1, 2), pltpu.roll(psi, 1, 2))
    chain_weights = (ce, 0.5 - ce, cn, 0.5 - cn)

    for m in range(SLICES - 1):
        @pl.when(n != m)
        def _():
            gap_copy(m, m).wait_recv()

    gathers = []
    for at, j in enumerate(offsets):
        count = SLICES + 1 - 2 * abs(j)
        gathers.append(
            pltpu.make_async_remote_copy(
                src_ref=pay.at[pl.ds(0, count), middle],
                dst_ref=pay.at[pl.ds(0, count), pl.ds(CROWS * (REACH - j), CROWS)],
                send_sem=b_send.at[at],
                recv_sem=b_recv.at[at],
                device_id=at_space(j),
                device_id_type=MESH,
            )
        )
        gathers[-1].start()
    for gather in gathers:
        gather.wait_recv()

    def new_copy(i, k):
        return pltpu.make_async_remote_copy(
            src_ref=nbuf.at[i, middle],
            dst_ref=newc.at[k],
            send_sem=c_send.at[i],
            recv_sem=c_recv.at[k],
            device_id=(i, b),
            device_id_type=MESH,
        )

    def link(i, current):
        t = current
        for s in range(4):
            change = operator(t, pltpu.roll(t, LANES - 1, 2), pltpu.roll(t, 1, 2), *chain_weights)
            if s == 0:
                change = COARSE_START * change
            t = COARSE_BETAS[s] * current + change
        for r in range(8):
            nbuf[i, pl.ds(4 + r, 8, stride=8)] = t[r]

        @pl.when(i != n)
        def _():
            new_copy(i, n).start()

        @pl.when(i == n)
        def _():
            newc[n] = nbuf[i, middle]

        late = lax.rem(i, SLICES - 1)
        return t + jnp.stack([pay[late, pl.ds(4 + r, 8, stride=8)] for r in range(8)])

    first = jnp.stack([pay[0, pl.ds(4 + r, 8, stride=8)] for r in range(8)])
    lax.fori_loop(1, SLICES, link, first)

    for k in range(SLICES):
        @pl.when((n != k) & (n > 0))
        def _():
            new_copy(k, k).wait_recv()

    lane = lax.broadcasted_iota(jnp.int32, (CROWS, LANES), 1)
    for c in range(CT):
        cbuf[c, pl.ds(8, CROWS)] = jnp.where(
            lane < LANES // 2, pltpu.roll(newc[2 * c], LANES - 32, 1), pltpu.roll(newc[2 * c + 1], 32, 1)
        )
    parts = []
    for c in range(CT):
        for q in range(2):
            new = cbuf[c, pl.ds(4 + q, 8, stride=2)]
            new = jnp.where(n == 0, old[c][q], new)
            parts.append(new - old[c][q])
    rows[...] = matmul(jnp.concatenate(parts, axis=0), grow[...])
    for c in range(CT):
        for m in range(4):
            t = base[4 * c + m]
            for r in range(8):
                xrows[pl.ds((4 * c + m) * 8 + r, 8, stride=FT * 8)] = (
                    t[r] + rows[pl.ds(8 * (2 * c + r // 4), 8), pl.ds(m * LANES, LANES)]
                )
    result = pltpu.make_async_copy(xwin.at[pl.ds(HALO // 8, BAND // 8)], out, local_sem.at[0])
    result.start()

    for halo in halos:
        halo.wait_send()
    for k in range(SLICES):
        @pl.when((n != k) & (n < SLICES - 1))
        def _():
            gap_copy(k, n).wait_send()
    for gather in gathers:
        gather.wait_send()
    for i in range(1, SLICES):
        @pl.when(n != i)
        def _():
            new_copy(i, n).wait_send()
    result.wait()


def per_device(states, stream):
    tiles = pltpu.VMEM((FT, 8, 8, LANES), F32)

    def tiled(x):
        return x.reshape(BAND // 8, 8, FT, LANES).transpose(0, 2, 1, 3)

    ended = pl.pallas_call(
        kernel,
        out_shape=jax.ShapeDtypeStruct((BAND // 8, FT, 8, LANES), F32),
        in_specs=[pl.BlockSpec(memory_space=pl.ANY)] * 2,
        out_specs=pl.BlockSpec(memory_space=pl.ANY),
        scratch_shapes=[
            pltpu.VMEM((WIDE // 8, FT, 8, LANES), F32),
            pltpu.VMEM((WIDE // 8, FT, 8, LANES), F32),
            tiles, tiles, tiles, tiles, tiles, tiles, tiles,
            pltpu.VMEM((4 * LANES, LANES), F32),
            pltpu.VMEM((LANES, 4 * LANES), F32),
            pltpu.VMEM((2 * CT * 8, 4 * LANES), F32),
            pltpu.VMEM((CT, 24, LANES), F32),
            pltpu.VMEM((SLICES, CROWS, LANES), F32),
            pltpu.VMEM((SLICES, CROWS, LANES), F32),
            pltpu.VMEM((CWIDE, LANES), F32),
            pltpu.VMEM((SLICES - 1, CWIDE, LANES), F32),
            pltpu.VMEM((SLICES, CWIDE, LANES), F32),
            pltpu.VMEM((SLICES, CROWS, LANES), F32),
            pltpu.SemaphoreType.DMA((2,)),
            pltpu.SemaphoreType.DMA((4,)),
            pltpu.SemaphoreType.DMA((4,)),
            pltpu.SemaphoreType.DMA((2 * REACH,)),
            pltpu.SemaphoreType.DMA((2 * REACH,)),
            pltpu.SemaphoreType.DMA((SLICES,)),
            pltpu.SemaphoreType.DMA((SLICES,)),
            pltpu.SemaphoreType.DMA((2 * REACH,)),
            pltpu.SemaphoreType.DMA((2 * REACH,)),
            pltpu.SemaphoreType.DMA((SLICES,)),
            pltpu.SemaphoreType.DMA((SLICES,)),
        ],
        compiler_params=pltpu.CompilerParams(
            collective_id=0, has_side_effects=True, vmem_limit_bytes=63 * 1024 * 1024
        ),
    )(tiled(states), tiled(stream))
    return ended.transpose(0, 2, 1, 3).reshape(1, BAND, COLS)


def solution(mesh):
    in_specs = (P("cuts", "space", None), P("space", None))
    out_specs = P("cuts", "space", None)
    return jax.shard_map(
        per_device, mesh=mesh, in_specs=in_specs, out_specs=out_specs, check_vma=False
    )
```

```python
import jax
import jax.numpy as jnp
from jax import lax
from jax.experimental import pallas as pl
from jax.experimental.pallas import tpu as pltpu
from jax.sharding import PartitionSpec as P

MESH = pl.DeviceIdType.MESH
LANES = 128
COLS = 2048
FT = COLS // LANES
CT = FT // 4
BAND = 32
HALO = 16
WIDE = BAND + 2 * HALO
SLICES = 8
SPACE = 16
REACH = 4
CROWS = 8
CWIDE = CROWS * (2 * REACH + 1)
FINE_STEPS = 4
GROUP = 4
F32 = jnp.float32


def scales(step, kappa):
    gains = [step / (4 - s) / kappa for s in range(4)]
    betas = [1.0] * 4
    for s in (2, 1, 0):
        betas[s] = betas[s + 1] * gains[s + 1]
    return betas, betas[0] * gains[0]


FINE_BETAS, FINE_START = scales(0.25, 1.25)
COARSE_BETAS, COARSE_START = scales(1.0, 20.0)


def rows_up(t):
    return jnp.concatenate([t[1:], pltpu.roll(t[:1], 7, 1)], axis=0)


def rows_down(t):
    return jnp.concatenate([pltpu.roll(t[-1:], 1, 1), t[:-1]], axis=0)


def columns(left, t, right):
    lane = lax.broadcasted_iota(jnp.int32, t.shape, 2)
    west = jnp.where(lane == 0, pltpu.roll(left, 1, 2), pltpu.roll(t, 1, 2))
    east = jnp.where(lane == LANES - 1, pltpu.roll(right, LANES - 1, 2), pltpu.roll(t, LANES - 1, 2))
    return east, west


def coefficients(psi, east, west):
    ce = 0.25 - 0.3125 * (rows_up(psi) - rows_down(psi))
    cn = 0.25 + 0.3125 * (east - west)
    return ce, cn


def operator(t, east, west, ce, cw, cn, cs):
    return ce * east + cw * west + cn * rows_up(t) + cs * rows_down(t) - t


def matmul(x, m):
    high = x.astype(jnp.bfloat16)
    x = x - high.astype(F32)
    middle = x.astype(jnp.bfloat16)
    low = (x - middle.astype(F32)).astype(jnp.bfloat16)
    small = jnp.dot(low, m, preferred_element_type=F32) + jnp.dot(middle, m, preferred_element_type=F32)
    return jnp.dot(high, m, preferred_element_type=F32) + small


def kernel(
    states, stream, out,
    xwin, swin, base, ta, tb, fce, fcw, fcn, fcs, shrink, grow, rows, cbuf, wstream, wgap, spw, pay, nbuf, newc, spread_rows,
    local_sem, halo_send, halo_recv, sc_send, sc_recv, a_send, a_recv, b_send, b_recv, c_send, c_recv,
):
    n = lax.axis_index("cuts")
    b = lax.axis_index("space")

    def flipped(k, bit):
        return k + bit * (1 - 2 * lax.rem(k, 2))

    side = lax.rem(b // 2, 2)
    column = flipped(n, side)

    def at_space(j):
        return (n, lax.rem(b + (SPACE + j), SPACE))

    def at_window(j):
        other = lax.rem(b + (SPACE + j), SPACE)
        return (flipped(n, lax.rem(side + lax.rem(other // 2, 2), 2)), other)

    across = 2 * lax.rem(b, 2) - 1

    offsets = [j for d in range(1, REACH + 1) for j in (-d, d)]

    own_x = pltpu.make_async_copy(states, xwin.at[pl.ds(HALO // 8, BAND // 8)], local_sem.at[0])
    own_s = pltpu.make_async_copy(stream, swin.at[pl.ds(HALO // 8, BAND // 8)], local_sem.at[1])
    xrows = xwin.reshape(WIDE * FT, LANES)
    srows = swin.reshape(WIDE * FT, LANES)
    own_s.start()
    own_x.start()

    pay[...] = jnp.zeros_like(pay)
    newc[...] = jnp.zeros_like(newc)

    barrier = pltpu.get_barrier_semaphore()
    greeted = [at_space(across)]
    greeted += [(lax.rem(n + k, SLICES), b) for k in range(1, SLICES)]
    greeted += [at_window(j) for j in reversed(offsets)]
    for device in greeted:
        pl.semaphore_signal(barrier, inc=1, device_id=device, device_id_type=MESH)
    pl.semaphore_wait(barrier, len(greeted))

    halos = []
    for at, (source, window, device) in enumerate(((stream, swin, at_window), (states, xwin, at_space))):
        for end, (j, first, target) in enumerate(((1, BAND - HALO, 0), (-1, 0, HALO + BAND))):
            halos.append(
                pltpu.make_async_remote_copy(
                    src_ref=source.at[pl.ds(first // 8, HALO // 8)],
                    dst_ref=window.at[pl.ds(target // 8, HALO // 8)],
                    send_sem=halo_send.at[2 * at + end],
                    recv_sem=halo_recv.at[2 * at + end],
                    device_id=device(j),
                    device_id_type=MESH,
                )
            )
            halos[-1].start()

    fine_at = lax.broadcasted_iota(jnp.int32, (4 * LANES, LANES), 0)
    coarse_at = lax.broadcasted_iota(jnp.int32, (4 * LANES, LANES), 1)
    shrink[...] = jnp.where((fine_at >> 2) == coarse_at, 0.0625, 0.0).astype(jnp.bfloat16)
    fine_at = lax.broadcasted_iota(jnp.int32, (LANES, 4 * LANES), 1)
    coarse_at = lax.broadcasted_iota(jnp.int32, (LANES, 4 * LANES), 0)
    grow[...] = jnp.where((fine_at >> 2) == coarse_at, 1.0, 0.0).astype(jnp.bfloat16)

    def windows(tiles, target):
        lane = lax.broadcasted_iota(jnp.int32, (CROWS, LANES), 1)
        right = [pltpu.roll(t, 32, 1) for t in tiles]
        left = [pltpu.roll(t, LANES - 32, 1) for t in tiles]
        for j in range(CT):
            target[2 * j] = jnp.where(lane < 32, right[(j - 1) % CT], right[j])
            target[2 * j + 1] = jnp.where(lane < LANES - 32, left[j], left[(j + 1) % CT])

    own_s.wait()
    for c in range(CT):
        for m in range(4):
            for half in range(2):
                parts = [srows[pl.ds(2 * FT * 8 + (4 * c + m) * 8 + 4 * half + i, 4, stride=FT * 8)] for i in range(4)]
                rows[pl.ds(8 * c + 4 * half, 4), pl.ds(m * LANES, LANES)] = parts[0] + parts[1] + parts[2] + parts[3]
    small = matmul(rows[pl.ds(0, CROWS * CT)], shrink[...])
    for c in range(CT):
        for half in range(2):
            cbuf[c, pl.ds(half, 4, stride=2)] = small[8 * c + 4 * half:8 * c + 4 * half + 4]
    windows([cbuf[c, pl.ds(0, CROWS)] for c in range(CT)], wstream)
    spreads = []
    for at, j in enumerate(offsets):
        spreads.append(
            pltpu.make_async_remote_copy(
                src_ref=wstream.at[column],
                dst_ref=spw.at[pl.ds(CROWS * (REACH - j), CROWS)],
                send_sem=sc_send.at[at],
                recv_sem=sc_recv.at[at],
                device_id=at_window(j),
                device_id_type=MESH,
            )
        )
        spreads[-1].start()
    spw[pl.ds(CROWS * REACH, CROWS)] = wstream[column]
    own_x.wait()

    for halo in halos[:2]:
        halo.wait_recv()

    def window_tile(window, c):
        return jnp.stack(
            [window[pl.ds(c * 8 + r, 8, stride=FT * 8)] for r in range(8)]
        )

    def add_rows(c, t):
        for q in range(2):
            rows[pl.ds(8 * (2 * (c // 4) + q), 8), pl.ds(c % 4 * LANES, LANES)] = (
                t[4 * q] + t[4 * q + 1] + (t[4 * q + 2] + t[4 * q + 3])
            )

    def restricted():
        small = matmul(rows[...], shrink[...])
        return [
            jnp.stack([small[8 * (2 * c + q):8 * (2 * c + q + 1)] for q in range(2)]) for c in range(CT)
        ]

    lane = lax.broadcasted_iota(jnp.int32, (8, 8, LANES), 2)
    west_before = pltpu.roll(window_tile(srows, FT - 1), 1, 2)
    psi = window_tile(srows, 0)
    east_now = pltpu.roll(psi, LANES - 1, 2)
    for c in range(FT):
        after = window_tile(srows, (c + 1) % FT)
        west_now, east_after = pltpu.roll(psi, 1, 2), pltpu.roll(after, LANES - 1, 2)
        ce, cn = coefficients(
            psi,
            jnp.where(lane == LANES - 1, east_after, east_now),
            jnp.where(lane == 0, west_before, west_now),
        )
        fce[c] = ce
        fcw[c] = 0.5 - ce
        fcn[c] = cn
        fcs[c] = 0.5 - cn
        add_rows(c, psi)
        psi, west_before, east_now = after, west_now, east_after

    cpsi = restricted()
    cweights = []
    for c in range(CT):
        east, west = columns(cpsi[c - 1], cpsi[c], cpsi[(c + 1) % CT])
        ce, cn = coefficients(cpsi[c], east, west)
        cweights.append((ce, 0.5 - ce, cn, 0.5 - cn))

    for halo in halos[2:]:
        halo.wait_recv()
    for c in range(FT):
        t = window_tile(xrows, c)
        base[c] = t
        add_rows(c, t)

    start = restricted()
    old = start
    for s in range(4):
        moved = []
        for c in range(CT):
            east, west = columns(old[c - 1], old[c], old[(c + 1) % CT])
            change = operator(old[c], east, west, *cweights[c])
            if s == 0:
                change = COARSE_START * change
            moved.append(COARSE_BETAS[s] * start[c] + change)
        old = moved

    def fine_stage(s, src, dst):
        lane = lax.broadcasted_iota(jnp.int32, (GROUP, 8, LANES), 2)

        def west_of(t):
            return pltpu.roll(t, 1, 2)

        def east_of(t):
            return pltpu.roll(t, LANES - 1, 2)

        for first in range(0, 8, GROUP):
            part = pl.ds(first, GROUP)
            west_before = west_of(src[FT - 1, part])
            t = src[0, part]
            east_now = east_of(t)
            for c in range(FT):
                after = src[(c + 1) % FT, part]
                west_now, east_after = west_of(t), east_of(after)
                west = jnp.where(lane == 0, west_before, west_now)
                east = jnp.where(lane == LANES - 1, east_after, east_now)
                if first + GROUP < 8:
                    above = src[c, pl.ds(first + GROUP, 1)]
                else:
                    above = pltpu.roll(src[c, pl.ds(0, 1)], 7, 1)
                if first > 0:
                    below = src[c, pl.ds(first - 1, 1)]
                else:
                    below = pltpu.roll(src[c, pl.ds(7, 1)], 1, 1)
                up = jnp.concatenate([t[1:], above], axis=0)
                down = jnp.concatenate([below, t[:-1]], axis=0)
                change = (fcn[c, part] * up + fcs[c, part] * down - t) + (
                    fce[c, part] * east + fcw[c, part] * west
                )
                if s == 0:
                    change = FINE_START * change
                dst[c, part] = FINE_BETAS[s] * base[c, part] + change
                t, west_before, east_now = after, west_now, east_after

    def fine_step(step, carry):
        fine_stage(0, base, ta)
        fine_stage(1, ta, tb)
        fine_stage(2, tb, ta)
        fine_stage(3, ta, base)
        return carry

    lax.fori_loop(0, FINE_STEPS, fine_step, 0)

    for c in range(FT):
        add_rows(c, base[c])
    ended = restricted()
    gap = [ended[c] - old[c] for c in range(CT)]
    gap = [jnp.where(n == 0, old[c] + gap[c], gap[c]) for c in range(CT)]
    for c in range(CT):
        for q in range(2):
            cbuf[c, pl.ds(4 + q, 8, stride=2)] = gap[c][q]
    windows([cbuf[c, pl.ds(8, CROWS)] for c in range(CT)], wgap)

    middle = pl.ds(CROWS * REACH, CROWS)

    def gap_copy(k, m):
        return pltpu.make_async_remote_copy(
            src_ref=wgap.at[flipped(k, side)],
            dst_ref=pay.at[m, middle],
            send_sem=a_send.at[k],
            recv_sem=a_recv.at[m],
            device_id=(k, b),
            device_id_type=MESH,
        )

    for k in range(SLICES):
        @pl.when((n != k) & (n < SLICES - 1))
        def _():
            gap_copy(k, n).start()

    @pl.when(n < SLICES - 1)
    def _():
        pay[n, middle] = wgap[column]

    for spread in spreads:
        spread.wait()
    psi = jnp.stack([spw[pl.ds(4 + r, 8, stride=8)] for r in range(8)])
    ce, cn = coefficients(psi, pltpu.roll(psi, LANES - 1, 2), pltpu.roll(psi, 1, 2))
    chain_weights = (ce, 0.5 - ce, cn, 0.5 - cn)

    for m in range(SLICES - 1):
        @pl.when(n != m)
        def _():
            gap_copy(m, m).wait_recv()

    gathers = []
    for at, j in enumerate(offsets):
        count = SLICES + 1 - 2 * abs(j)
        gathers.append(
            pltpu.make_async_remote_copy(
                src_ref=pay.at[pl.ds(0, count), middle],
                dst_ref=pay.at[pl.ds(0, count), pl.ds(CROWS * (REACH - j), CROWS)],
                send_sem=b_send.at[at],
                recv_sem=b_recv.at[at],
                device_id=at_window(j),
                device_id_type=MESH,
            )
        )
        gathers[-1].start()

    for c in range(FT):
        t = base[c]
        for r in range(8):
            xrows[pl.ds(c * 8 + r, 8, stride=FT * 8)] = t[r]
    for c in range(CT):
        for q in range(2):
            cbuf[c, pl.ds(4 + q, 8, stride=2)] = old[c][q]

    for gather in gathers:
        gather.wait_recv()

    def new_copy(i, window):
        return pltpu.make_async_remote_copy(
            src_ref=nbuf.at[i, middle],
            dst_ref=newc.at[window],
            send_sem=c_send.at[i],
            recv_sem=c_recv.at[window],
            device_id=(i, b),
            device_id_type=MESH,
        )

    def link(i, current):
        t = current
        for s in range(4):
            change = operator(t, pltpu.roll(t, LANES - 1, 2), pltpu.roll(t, 1, 2), *chain_weights)
            if s == 0:
                change = COARSE_START * change
            t = COARSE_BETAS[s] * current + change
        for r in range(8):
            nbuf[i, pl.ds(4 + r, 8, stride=8)] = t[r]

        @pl.when(i != n)
        def _():
            new_copy(i, column).start()

        @pl.when(i == n)
        def _():
            newc[column] = nbuf[i, middle]

        late = lax.rem(i, SLICES - 1)
        return t + jnp.stack([pay[late, pl.ds(4 + r, 8, stride=8)] for r in range(8)])

    first = jnp.stack([pay[0, pl.ds(4 + r, 8, stride=8)] for r in range(8)])
    lax.fori_loop(1, SLICES, link, first)

    for k in range(SLICES):
        @pl.when((n != k) & (n > 0))
        def _():
            new_copy(k, flipped(k, side)).wait_recv()

    lane = lax.broadcasted_iota(jnp.int32, (CROWS, LANES), 1)
    for c in range(CT):
        new = jnp.where(
            lane < LANES // 2, pltpu.roll(newc[2 * c], LANES - 32, 1), pltpu.roll(newc[2 * c + 1], 32, 1)
        )
        was = cbuf[c, pl.ds(8, CROWS)]
        change = jnp.where(n == 0, was, new) - was
        for i in range(4):
            spread_rows[pl.ds(BAND * c + i, CROWS, stride=4)] = change
    fine_change = matmul(spread_rows[...], grow[...])
    for c in range(CT):
        for m in range(4):
            for i in range(BAND // 8):
                out[i, 4 * c + m] = (
                    xwin[HALO // 8 + i, 4 * c + m]
                    + fine_change[BAND * c + 8 * i:BAND * c + 8 * (i + 1), m * LANES:(m + 1) * LANES]
                )

    for halo in halos:
        halo.wait_send()
    for k in range(SLICES):
        @pl.when((n != k) & (n < SLICES - 1))
        def _():
            gap_copy(k, n).wait_send()
    for gather in gathers:
        gather.wait_send()
    for i in range(1, SLICES):
        @pl.when(n != i)
        def _():
            new_copy(i, column).wait_send()


def per_device(states, stream):
    tiles = pltpu.VMEM((FT, 8, 8, LANES), F32)

    def tiled(x):
        return x.reshape(BAND // 8, 8, FT, LANES).transpose(0, 2, 1, 3)

    ended = pl.pallas_call(
        kernel,
        out_shape=pltpu.VMEM((BAND // 8, FT, 8, LANES), F32),
        in_specs=[pl.BlockSpec(memory_space=pl.ANY)] * 2,
        out_specs=pl.BlockSpec(memory_space=pltpu.VMEM),
        scratch_shapes=[
            pltpu.VMEM((WIDE // 8, FT, 8, LANES), F32),
            pltpu.VMEM((WIDE // 8, FT, 8, LANES), F32),
            tiles, tiles, tiles, tiles, tiles, tiles, tiles,
            pltpu.VMEM((4 * LANES, LANES), jnp.bfloat16),
            pltpu.VMEM((LANES, 4 * LANES), jnp.bfloat16),
            pltpu.VMEM((2 * CT * 8, 4 * LANES), F32),
            pltpu.VMEM((CT, 24, LANES), F32),
            pltpu.VMEM((SLICES, CROWS, LANES), F32),
            pltpu.VMEM((SLICES, CROWS, LANES), F32),
            pltpu.VMEM((CWIDE, LANES), F32),
            pltpu.VMEM((SLICES - 1, CWIDE, LANES), F32),
            pltpu.VMEM((SLICES, CWIDE, LANES), F32),
            pltpu.VMEM((SLICES, CROWS, LANES), F32),
            pltpu.VMEM((CT * BAND, LANES), F32),
            pltpu.SemaphoreType.DMA((2,)),
            pltpu.SemaphoreType.DMA((4,)),
            pltpu.SemaphoreType.DMA((4,)),
            pltpu.SemaphoreType.DMA((2 * REACH,)),
            pltpu.SemaphoreType.DMA((2 * REACH,)),
            pltpu.SemaphoreType.DMA((SLICES,)),
            pltpu.SemaphoreType.DMA((SLICES,)),
            pltpu.SemaphoreType.DMA((2 * REACH,)),
            pltpu.SemaphoreType.DMA((2 * REACH,)),
            pltpu.SemaphoreType.DMA((SLICES,)),
            pltpu.SemaphoreType.DMA((SLICES,)),
        ],
        compiler_params=pltpu.CompilerParams(
            collective_id=0, has_side_effects=True, vmem_limit_bytes=60 * 1024 * 1024
        ),
    )(tiled(states), tiled(stream))
    return ended.transpose(0, 2, 1, 3).reshape(1, BAND, COLS)


def solution(mesh):
    in_specs = (P("cuts", "space", None), P("space", None))
    out_specs = P("cuts", "space", None)
    return jax.shard_map(
        per_device, mesh=mesh, in_specs=in_specs, out_specs=out_specs, check_vma=False
    )
```

```python
import jax
import jax.numpy as jnp
from jax import lax
from jax.experimental import pallas as pl
from jax.experimental.pallas import tpu as pltpu
from jax.sharding import PartitionSpec as P

MESH = pl.DeviceIdType.MESH
LANES = 128
COLS = 2048
FT = COLS // LANES
CT = FT // 4
BAND = 32
HALO = 16
WIDE = BAND + 2 * HALO
SLICES = 8
SPACE = 16
REACH = 4
CROWS = 8
CWIDE = CROWS * (2 * REACH + 1)
FINE_STEPS = 4
SPAN = 4
STAGES = 4 * FINE_STEPS
F32 = jnp.float32


def scales(step, kappa):
    gains = [step / (4 - s) / kappa for s in range(4)]
    betas = [1.0] * 4
    for s in (2, 1, 0):
        betas[s] = betas[s + 1] * gains[s + 1]
    return betas, betas[0] * gains[0]


FINE_BETAS, FINE_START = scales(0.25, 1.25)
COARSE_BETAS, COARSE_START = scales(1.0, 20.0)


def rows_up(t):
    return jnp.concatenate([t[1:], pltpu.roll(t[:1], 7, 1)], axis=0)


def rows_down(t):
    return jnp.concatenate([pltpu.roll(t[-1:], 1, 1), t[:-1]], axis=0)


def coefficients(psi, east, west):
    ce = 0.25 - 0.3125 * (rows_up(psi) - rows_down(psi))
    cn = 0.25 + 0.3125 * (east - west)
    return ce, cn


def operator(t, east, west, ce, cw, cn, cs):
    return ce * east + cw * west + cn * rows_up(t) + cs * rows_down(t) - t


def matmul(x, m):
    high = x.astype(jnp.bfloat16)
    x = x - high.astype(F32)
    middle = x.astype(jnp.bfloat16)
    low = (x - middle.astype(F32)).astype(jnp.bfloat16)
    small = jnp.dot(low, m, preferred_element_type=F32) + jnp.dot(middle, m, preferred_element_type=F32)
    return jnp.dot(high, m, preferred_element_type=F32) + small


def kernel(
    states, stream, out,
    xwin, swin, psi, field, fce, fcn, shrink, grow, rows, cpsi, cce, ccn, cfield, wstream, wgap, spw, pay, nbuf, newc, spread_rows,
    local_sem, halo_send, halo_recv, sc_send, sc_recv, a_send, a_recv, b_send, b_recv, c_send, c_recv,
):
    n = lax.axis_index("cuts")
    b = lax.axis_index("space")

    def flipped(k, bit):
        return k + bit * (1 - 2 * lax.rem(k, 2))

    side = lax.rem(b // 2, 2)
    column = flipped(n, side)

    def at_space(j):
        return (n, lax.rem(b + (SPACE + j), SPACE))

    def at_window(j):
        other = lax.rem(b + (SPACE + j), SPACE)
        return (flipped(n, lax.rem(side + lax.rem(other // 2, 2), 2)), other)

    across = 2 * lax.rem(b, 2) - 1

    offsets = [j for d in range(1, REACH + 1) for j in (-d, d)]

    own_x = pltpu.make_async_copy(states, xwin.at[pl.ds(HALO // 8, BAND // 8)], local_sem.at[0])
    own_s = pltpu.make_async_copy(stream, swin.at[pl.ds(HALO // 8, BAND // 8)], local_sem.at[1])
    own_s.start()
    own_x.start()

    pay[...] = jnp.zeros_like(pay)
    newc[...] = jnp.zeros_like(newc)

    barrier = pltpu.get_barrier_semaphore()
    greeted = [at_space(across)]
    greeted += [(lax.rem(n + k, SLICES), b) for k in range(1, SLICES)]
    greeted += [at_window(j) for j in reversed(offsets)]
    for device in greeted:
        pl.semaphore_signal(barrier, inc=1, device_id=device, device_id_type=MESH)
    pl.semaphore_wait(barrier, len(greeted))

    halos = []
    for at, (source, window, device) in enumerate(((stream, swin, at_window), (states, xwin, at_space))):
        for end, (j, first, target) in enumerate(((1, BAND - HALO, 0), (-1, 0, HALO + BAND))):
            halos.append(
                pltpu.make_async_remote_copy(
                    src_ref=source.at[pl.ds(first // 8, HALO // 8)],
                    dst_ref=window.at[pl.ds(target // 8, HALO // 8)],
                    send_sem=halo_send.at[2 * at + end],
                    recv_sem=halo_recv.at[2 * at + end],
                    device_id=device(j),
                    device_id_type=MESH,
                )
            )
            halos[-1].start()

    fine_at = lax.broadcasted_iota(jnp.int32, (4 * LANES, LANES), 0)
    coarse_at = lax.broadcasted_iota(jnp.int32, (4 * LANES, LANES), 1)
    shrink[...] = jnp.where((fine_at >> 2) == coarse_at, 0.0625, 0.0).astype(jnp.bfloat16)
    fine_at = lax.broadcasted_iota(jnp.int32, (LANES, 4 * LANES), 1)
    coarse_at = lax.broadcasted_iota(jnp.int32, (LANES, 4 * LANES), 0)
    grow[...] = jnp.where((fine_at >> 2) == coarse_at, 1.0, 0.0).astype(jnp.bfloat16)

    def windows(tiles, target):
        lane = lax.broadcasted_iota(jnp.int32, (CROWS, LANES), 1)
        right = [pltpu.roll(t, 32, 1) for t in tiles]
        left = [pltpu.roll(t, LANES - 32, 1) for t in tiles]
        for j in range(CT):
            target[2 * j] = jnp.where(lane < 32, right[(j - 1) % CT], right[j])
            target[2 * j + 1] = jnp.where(lane < LANES - 32, left[j], left[(j + 1) % CT])

    own = range(HALO // 8, (HALO + BAND) // 8)
    around = [i for i in range(WIDE // 8) if i not in own]

    def untile(window, target, parts):
        for i in parts:
            for c in range(FT):
                target[c, pl.ds(8 * i, 8)] = window[i, c]

    def add_rows(source, at, first):
        for c in range(FT):
            parts = [source[c, pl.ds(first + i, 8, stride=4)] for i in range(4)]
            rows[pl.ds(at(c // 4), 8), pl.ds(c % 4 * LANES, LANES)] = parts[0] + parts[1] + (parts[2] + parts[3])

    def restricted_band(source):
        add_rows(source, lambda c: CROWS * c, HALO)
        small = matmul(rows[pl.ds(0, CROWS * CT)], shrink[...])
        return [small[CROWS * c:CROWS * (c + 1)] for c in range(CT)]

    def restricted_window(source, target):
        for half in range(2):
            add_rows(source, lambda c: 2 * CROWS * c + CROWS * half, half * WIDE // 2)
        small = matmul(rows[...], shrink[...])
        for c in range(CT):
            target[c] = small[2 * CROWS * c:2 * CROWS * (c + 1)]

    own_s.wait()
    untile(swin, psi, own)
    windows(restricted_band(psi), wstream)
    spreads = []
    for at, j in enumerate(offsets):
        spreads.append(
            pltpu.make_async_remote_copy(
                src_ref=wstream.at[column],
                dst_ref=spw.at[pl.ds(CROWS * (REACH - j), CROWS)],
                send_sem=sc_send.at[at],
                recv_sem=sc_recv.at[at],
                device_id=at_window(j),
                device_id_type=MESH,
            )
        )
        spreads[-1].start()
    spw[pl.ds(CROWS * REACH, CROWS)] = wstream[column]
    own_x.wait()

    def first_lane(t):
        return lax.broadcasted_iota(jnp.int32, t.shape, 1) == 0

    def last_lane(t):
        return lax.broadcasted_iota(jnp.int32, t.shape, 1) == LANES - 1

    def wrapped(c):
        return c % FT if isinstance(c, int) else lax.rem(c, FT)

    def over_tiles(source, blocks, tiles, work):
        def west_of(c):
            return [pltpu.roll(source[c, pl.ds(*block)], 1, 1) for block in blocks]

        def east_of(c):
            return [pltpu.roll(source[c, pl.ds(*block)], LANES - 1, 1) for block in blocks]

        before, now = west_of(wrapped(tiles[0] + FT - 1)), east_of(tiles[0])
        for c in tiles:
            west_now, after = west_of(c), east_of(wrapped(c + 1))
            for i, block in enumerate(blocks):
                t = source[c, pl.ds(*block)]
                west = jnp.where(first_lane(t), before[i], west_now[i])
                east = jnp.where(last_lane(t), after[i], now[i])
                work(c, block, t, east, west)
            before, now = west_now, after

    def shifted(source, c, block, by):
        return source[c, pl.ds(block[0] + by, block[1])]

    def weigh(c, block, t, east, west):
        fce[c, pl.ds(*block)] = 0.25 - 0.3125 * (shifted(psi, c, block, 1) - shifted(psi, c, block, -1))
        fcn[c, pl.ds(*block)] = 0.25 + 0.3125 * (east - west)

    def stage(at, base_at, s, blocks, tiles):
        source, base, target = field.at[at], field.at[base_at], field.at[at + 1]

        def work(c, block, t, east, west):
            here = pl.ds(*block)
            up, down = shifted(source, c, block, 1), shifted(source, c, block, -1)
            change = fcn[c, here] * (up - down) + (0.5 * (west + down) - t) + fce[c, here] * (east - west)
            if s == 0:
                change = FINE_START * change
            target[c, here] = FINE_BETAS[s] * base[c, here] + change

        over_tiles(source, blocks, tiles, work)

    def blocks_of(first, last):
        count = max((last - first + 7) // 8, 1)
        return [(first + 8 * i, 8) for i in range(count - 1)] + [(max(last - 8, first), 8)]

    def by_runs(work):
        def run(at, carry):
            work([at * SPAN + i for i in range(SPAN)])
            return carry

        lax.fori_loop(0, FT // SPAN, run, 0)

    untile(xwin, field.at[0], own)
    by_runs(lambda tiles: over_tiles(psi, blocks_of(HALO + 1, HALO + BAND - 1), tiles, weigh))
    for k in range(STAGES - 1):
        inner = blocks_of(HALO + k + 1, HALO + BAND - k - 1)
        by_runs(lambda tiles: stage(k, k // 4 * 4, k % 4, inner, tiles))

    for halo in halos[:2]:
        halo.wait_recv()
    untile(swin, psi, around)
    over_tiles(psi, [(1, HALO), (WIDE - 1 - HALO, HALO)], range(FT), weigh)
    restricted_window(psi, cpsi)
    middle_rows = [(1, 8), (7, 8)]
    for c in range(CT):
        for block in middle_rows:
            t = [cpsi[(c + d) % CT, pl.ds(*block)] for d in (-1, 0, 1)]
            west = jnp.where(first_lane(t[1]), pltpu.roll(t[0], 1, 1), pltpu.roll(t[1], 1, 1))
            east = jnp.where(last_lane(t[1]), pltpu.roll(t[2], LANES - 1, 1), pltpu.roll(t[1], LANES - 1, 1))
            cce[c, pl.ds(*block)] = 0.25 - 0.3125 * (shifted(cpsi, c, block, 1) - shifted(cpsi, c, block, -1))
            ccn[c, pl.ds(*block)] = 0.25 + 0.3125 * (east - west)

    for halo in halos[2:]:
        halo.wait_recv()
    untile(xwin, field.at[0], around)

    restricted_window(field.at[0], cfield.at[0])
    for s in range(4):
        for c in range(CT):
            for block in [(s + 1, 8), (7 - s, 8)][:2 if s < 3 else 1]:
                here = pl.ds(*block)
                t = [cfield[s, (c + d) % CT, here] for d in (-1, 0, 1)]
                west = jnp.where(first_lane(t[1]), pltpu.roll(t[0], 1, 1), pltpu.roll(t[1], 1, 1))
                east = jnp.where(last_lane(t[1]), pltpu.roll(t[2], LANES - 1, 1), pltpu.roll(t[1], LANES - 1, 1))
                up, down = shifted(cfield.at[s], c, block, 1), shifted(cfield.at[s], c, block, -1)
                change = ccn[c, here] * (up - down) + (0.5 * (west + down) - t[1]) + cce[c, here] * (east - west)
                if s == 0:
                    change = COARSE_START * change
                cfield[s + 1, c, here] = COARSE_BETAS[s] * cfield[0, c, here] + change
    coarse_old = [cfield.at[4, c, pl.ds(4, CROWS)] for c in range(CT)]

    def fine_step(step, carry):
        for s in range(4):
            done = 4 * step + s
            blocks = [(done + 1, HALO), (WIDE - HALO - 1 - done, HALO)]
            stage(done, 4 * step, s, blocks, range(FT))
        return carry

    lax.fori_loop(0, FINE_STEPS, fine_step, 0)
    fine_end = field.at[STAGES]

    ended = restricted_band(fine_end)
    gap = [ended[c] - coarse_old[c][...] for c in range(CT)]
    windows([jnp.where(n == 0, coarse_old[c][...] + gap[c], gap[c]) for c in range(CT)], wgap)

    middle = pl.ds(CROWS * REACH, CROWS)

    def gap_copy(k, m):
        return pltpu.make_async_remote_copy(
            src_ref=wgap.at[flipped(k, side)],
            dst_ref=pay.at[m, middle],
            send_sem=a_send.at[k],
            recv_sem=a_recv.at[m],
            device_id=(k, b),
            device_id_type=MESH,
        )

    for k in range(SLICES):
        @pl.when((n != k) & (n < SLICES - 1))
        def _():
            gap_copy(k, n).start()

    @pl.when(n < SLICES - 1)
    def _():
        pay[n, middle] = wgap[column]

    for spread in spreads:
        spread.wait()
    around_psi = jnp.stack([spw[pl.ds(4 + r, 8, stride=8)] for r in range(8)])
    ce, cn = coefficients(
        around_psi, pltpu.roll(around_psi, LANES - 1, 2), pltpu.roll(around_psi, 1, 2)
    )
    chain_weights = (ce, 0.5 - ce, cn, 0.5 - cn)

    for m in range(SLICES - 1):
        @pl.when(n != m)
        def _():
            gap_copy(m, m).wait_recv()

    gathers = []
    for at, j in enumerate(offsets):
        count = SLICES + 1 - 2 * abs(j)
        gathers.append(
            pltpu.make_async_remote_copy(
                src_ref=pay.at[pl.ds(0, count), middle],
                dst_ref=pay.at[pl.ds(0, count), pl.ds(CROWS * (REACH - j), CROWS)],
                send_sem=b_send.at[at],
                recv_sem=b_recv.at[at],
                device_id=at_window(j),
                device_id_type=MESH,
            )
        )
        gathers[-1].start()

    for gather in gathers:
        gather.wait_recv()

    def new_copy(i, window):
        return pltpu.make_async_remote_copy(
            src_ref=nbuf.at[i, middle],
            dst_ref=newc.at[window],
            send_sem=c_send.at[i],
            recv_sem=c_recv.at[window],
            device_id=(i, b),
            device_id_type=MESH,
        )

    def link(i, current):
        t = current
        for s in range(4):
            change = operator(t, pltpu.roll(t, LANES - 1, 2), pltpu.roll(t, 1, 2), *chain_weights)
            if s == 0:
                change = COARSE_START * change
            t = COARSE_BETAS[s] * current + change
        for r in range(8):
            nbuf[i, pl.ds(4 + r, 8, stride=8)] = t[r]

        @pl.when(i != n)
        def _():
            new_copy(i, column).start()

        @pl.when(i == n)
        def _():
            newc[column] = nbuf[i, middle]

        late = lax.rem(i, SLICES - 1)
        return t + jnp.stack([pay[late, pl.ds(4 + r, 8, stride=8)] for r in range(8)])

    first = jnp.stack([pay[0, pl.ds(4 + r, 8, stride=8)] for r in range(8)])
    lax.fori_loop(1, SLICES, link, first)

    for k in range(SLICES):
        @pl.when((n != k) & (n > 0))
        def _():
            new_copy(k, flipped(k, side)).wait_recv()

    lane = lax.broadcasted_iota(jnp.int32, (CROWS, LANES), 1)
    for c in range(CT):
        new = jnp.where(
            lane < LANES // 2, pltpu.roll(newc[2 * c], LANES - 32, 1), pltpu.roll(newc[2 * c + 1], 32, 1)
        )
        was = coarse_old[c][...]
        change = jnp.where(n == 0, was, new) - was
        for i in range(4):
            spread_rows[pl.ds(BAND * c + i, CROWS, stride=4)] = change
    fine_change = matmul(spread_rows[...], grow[...])
    for c in range(CT):
        for m in range(4):
            for i in range(BAND // 8):
                out[i, 4 * c + m] = (
                    fine_end[4 * c + m, pl.ds(HALO + 8 * i, 8)]
                    + fine_change[BAND * c + 8 * i:BAND * c + 8 * (i + 1), m * LANES:(m + 1) * LANES]
                )

    for halo in halos:
        halo.wait_send()
    for k in range(SLICES):
        @pl.when((n != k) & (n < SLICES - 1))
        def _():
            gap_copy(k, n).wait_send()
    for gather in gathers:
        gather.wait_send()
    for i in range(1, SLICES):
        @pl.when(n != i)
        def _():
            new_copy(i, column).wait_send()


def per_device(states, stream):
    fine = pltpu.VMEM((FT, WIDE, LANES), F32)
    coarse = pltpu.VMEM((CT, 2 * CROWS, LANES), F32)

    def tiled(x):
        return x.reshape(BAND // 8, 8, FT, LANES).transpose(0, 2, 1, 3)

    ended = pl.pallas_call(
        kernel,
        out_shape=pltpu.VMEM((BAND // 8, FT, 8, LANES), F32),
        in_specs=[pl.BlockSpec(memory_space=pl.ANY)] * 2,
        out_specs=pl.BlockSpec(memory_space=pltpu.VMEM),
        scratch_shapes=[
            pltpu.VMEM((WIDE // 8, FT, 8, LANES), F32),
            pltpu.VMEM((WIDE // 8, FT, 8, LANES), F32),
            fine,
            pltpu.VMEM((STAGES + 1, FT, WIDE, LANES), F32),
            fine,
            fine,
            pltpu.VMEM((4 * LANES, LANES), jnp.bfloat16),
            pltpu.VMEM((LANES, 4 * LANES), jnp.bfloat16),
            pltpu.VMEM((2 * CT * 8, 4 * LANES), F32),
            coarse,
            coarse,
            coarse,
            pltpu.VMEM((5, CT, 2 * CROWS, LANES), F32),
            pltpu.VMEM((SLICES, CROWS, LANES), F32),
            pltpu.VMEM((SLICES, CROWS, LANES), F32),
            pltpu.VMEM((CWIDE, LANES), F32),
            pltpu.VMEM((SLICES - 1, CWIDE, LANES), F32),
            pltpu.VMEM((SLICES, CWIDE, LANES), F32),
            pltpu.VMEM((SLICES, CROWS, LANES), F32),
            pltpu.VMEM((CT * BAND, LANES), F32),
            pltpu.SemaphoreType.DMA((2,)),
            pltpu.SemaphoreType.DMA((4,)),
            pltpu.SemaphoreType.DMA((4,)),
            pltpu.SemaphoreType.DMA((2 * REACH,)),
            pltpu.SemaphoreType.DMA((2 * REACH,)),
            pltpu.SemaphoreType.DMA((SLICES,)),
            pltpu.SemaphoreType.DMA((SLICES,)),
            pltpu.SemaphoreType.DMA((2 * REACH,)),
            pltpu.SemaphoreType.DMA((2 * REACH,)),
            pltpu.SemaphoreType.DMA((SLICES,)),
            pltpu.SemaphoreType.DMA((SLICES,)),
        ],
        compiler_params=pltpu.CompilerParams(
            collective_id=0, has_side_effects=True, vmem_limit_bytes=60 * 1024 * 1024
        ),
    )(tiled(states), tiled(stream))
    return ended.transpose(0, 2, 1, 3).reshape(1, BAND, COLS)


def solution(mesh):
    in_specs = (P("cuts", "space", None), P("space", None))
    out_specs = P("cuts", "space", None)
    return jax.shard_map(
        per_device, mesh=mesh, in_specs=in_specs, out_specs=out_specs, check_vma=False
    )
```

```python
import jax
import jax.numpy as jnp
from jax import lax
from jax.experimental import pallas as pl
from jax.experimental.pallas import tpu as pltpu
from jax.sharding import PartitionSpec as P

MESH = pl.DeviceIdType.MESH
LANES = 128
COLS = 2048
FT = COLS // LANES
CT = FT // 4
BAND = 32
HALO = 16
WIDE = BAND + 2 * HALO
SLICES = 8
SPACE = 16
REACH = 4
CROWS = 8
CWIDE = CROWS * (2 * REACH + 1)
FINE_STEPS = 4
SPAN = 4
STAGES = 4 * FINE_STEPS
F32 = jnp.float32


def scales(step, kappa):
    gains = [step / (4 - s) / kappa for s in range(4)]
    betas = [1.0] * 4
    for s in (2, 1, 0):
        betas[s] = betas[s + 1] * gains[s + 1]
    return betas, betas[0] * gains[0]


FINE_BETAS, FINE_START = scales(0.25, 1.25)
COARSE_BETAS, COARSE_START = scales(1.0, 20.0)


def rows_up(t):
    return jnp.concatenate([t[1:], pltpu.roll(t[:1], 7, 1)], axis=0)


def rows_down(t):
    return jnp.concatenate([pltpu.roll(t[-1:], 1, 1), t[:-1]], axis=0)


def coefficients(psi, east, west):
    ce = 0.25 - 0.3125 * (rows_up(psi) - rows_down(psi))
    cn = 0.25 + 0.3125 * (east - west)
    return ce, cn


def operator(t, east, west, ce, cw, cn, cs):
    return ce * east + cw * west + cn * rows_up(t) + cs * rows_down(t) - t


def matmul(x, m):
    high = x.astype(jnp.bfloat16)
    x = x - high.astype(F32)
    middle = x.astype(jnp.bfloat16)
    low = (x - middle.astype(F32)).astype(jnp.bfloat16)
    small = jnp.dot(low, m, preferred_element_type=F32) + jnp.dot(middle, m, preferred_element_type=F32)
    return jnp.dot(high, m, preferred_element_type=F32) + small


def kernel(
    states, stream, out,
    xwin, swin, psi, field, field1, field2, field3, fce, fcn, shrink, grow, rows, cpsi, cce, ccn, cfield, wstream, wgap, spw, pay, nbuf, newc, spread_rows,
    local_sem, halo_send, halo_recv, sc_send, sc_recv, a_send, a_recv, b_send, b_recv, c_send, c_recv,
):
    n = lax.axis_index("cuts")
    b = lax.axis_index("space")

    def flipped(k, bit):
        return k + bit * (1 - 2 * lax.rem(k, 2))

    side = lax.rem(b // 2, 2)
    column = flipped(n, side)

    def at_space(j):
        return (n, lax.rem(b + (SPACE + j), SPACE))

    def at_window(j):
        other = lax.rem(b + (SPACE + j), SPACE)
        return (flipped(n, lax.rem(side + lax.rem(other // 2, 2), 2)), other)

    across = 2 * lax.rem(b, 2) - 1

    offsets = [j for d in range(1, REACH + 1) for j in (-d, d)]

    own_x = pltpu.make_async_copy(states, xwin.at[pl.ds(HALO // 8, BAND // 8)], local_sem.at[0])
    own_s = pltpu.make_async_copy(stream, swin.at[pl.ds(HALO // 8, BAND // 8)], local_sem.at[1])
    own_s.start()
    own_x.start()

    pay[...] = jnp.zeros_like(pay)
    newc[...] = jnp.zeros_like(newc)

    barrier = pltpu.get_barrier_semaphore()
    greeted = [at_space(across)]
    greeted += [(lax.rem(n + k, SLICES), b) for k in range(1, SLICES)]
    greeted += [at_window(j) for j in reversed(offsets)]
    for device in greeted:
        pl.semaphore_signal(barrier, inc=1, device_id=device, device_id_type=MESH)
    pl.semaphore_wait(barrier, len(greeted))

    halos = []
    for at, (source, window, device) in enumerate(((stream, swin, at_window), (states, xwin, at_space))):
        for end, (j, first, target) in enumerate(((1, BAND - HALO, 0), (-1, 0, HALO + BAND))):
            halos.append(
                pltpu.make_async_remote_copy(
                    src_ref=source.at[pl.ds(first // 8, HALO // 8)],
                    dst_ref=window.at[pl.ds(target // 8, HALO // 8)],
                    send_sem=halo_send.at[2 * at + end],
                    recv_sem=halo_recv.at[2 * at + end],
                    device_id=device(j),
                    device_id_type=MESH,
                )
            )
            halos[-1].start()

    fine_at = lax.broadcasted_iota(jnp.int32, (4 * LANES, LANES), 0)
    coarse_at = lax.broadcasted_iota(jnp.int32, (4 * LANES, LANES), 1)
    shrink[...] = jnp.where((fine_at >> 2) == coarse_at, 0.0625, 0.0).astype(jnp.bfloat16)
    fine_at = lax.broadcasted_iota(jnp.int32, (LANES, 4 * LANES), 1)
    coarse_at = lax.broadcasted_iota(jnp.int32, (LANES, 4 * LANES), 0)
    grow[...] = jnp.where((fine_at >> 2) == coarse_at, 1.0, 0.0).astype(jnp.bfloat16)

    def windows(tiles, target):
        lane = lax.broadcasted_iota(jnp.int32, (CROWS, LANES), 1)
        right = [pltpu.roll(t, 32, 1) for t in tiles]
        left = [pltpu.roll(t, LANES - 32, 1) for t in tiles]
        for j in range(CT):
            target[2 * j] = jnp.where(lane < 32, right[(j - 1) % CT], right[j])
            target[2 * j + 1] = jnp.where(lane < LANES - 32, left[j], left[(j + 1) % CT])

    own = range(HALO // 8, (HALO + BAND) // 8)
    around = [i for i in range(WIDE // 8) if i not in own]

    def untile(window, target, parts):
        for i in parts:
            for c in range(FT):
                target[c, pl.ds(8 * i, 8)] = window[i, c]

    def add_rows(source, at, first):
        for c in range(FT):
            parts = [source[c, pl.ds(first + i, 8, stride=4)] for i in range(4)]
            rows[pl.ds(at(c // 4), 8), pl.ds(c % 4 * LANES, LANES)] = parts[0] + parts[1] + (parts[2] + parts[3])

    def restricted_band(source):
        add_rows(source, lambda c: CROWS * c, HALO)
        small = matmul(rows[pl.ds(0, CROWS * CT)], shrink[...])
        return [small[CROWS * c:CROWS * (c + 1)] for c in range(CT)]

    def restricted_window(source, target):
        for half in range(2):
            add_rows(source, lambda c: 2 * CROWS * c + CROWS * half, half * WIDE // 2)
        small = matmul(rows[...], shrink[...])
        for c in range(CT):
            target[c] = small[2 * CROWS * c:2 * CROWS * (c + 1)]

    own_s.wait()
    untile(swin, psi, own)
    windows(restricted_band(psi), wstream)
    spreads = []
    for at, j in enumerate(offsets):
        spreads.append(
            pltpu.make_async_remote_copy(
                src_ref=wstream.at[column],
                dst_ref=spw.at[pl.ds(CROWS * (REACH - j), CROWS)],
                send_sem=sc_send.at[at],
                recv_sem=sc_recv.at[at],
                device_id=at_window(j),
                device_id_type=MESH,
            )
        )
        spreads[-1].start()
    spw[pl.ds(CROWS * REACH, CROWS)] = wstream[column]
    own_x.wait()

    def first_lane(t):
        return lax.broadcasted_iota(jnp.int32, t.shape, 1) == 0

    def last_lane(t):
        return lax.broadcasted_iota(jnp.int32, t.shape, 1) == LANES - 1

    def wrapped(c):
        return c % FT if isinstance(c, int) else lax.rem(c, FT)

    def over_tiles(source, blocks, tiles, work):
        def west_of(c):
            return [pltpu.roll(source[c, pl.ds(*block)], 1, 1) for block in blocks]

        def east_of(c):
            return [pltpu.roll(source[c, pl.ds(*block)], LANES - 1, 1) for block in blocks]

        before, now = west_of(wrapped(tiles[0] + FT - 1)), east_of(tiles[0])
        for c in tiles:
            west_now, after = west_of(c), east_of(wrapped(c + 1))
            for i, block in enumerate(blocks):
                t = source[c, pl.ds(*block)]
                west = jnp.where(first_lane(t), before[i], west_now[i])
                east = jnp.where(last_lane(t), after[i], now[i])
                work(c, block, t, east, west)
            before, now = west_now, after

    def shifted(source, c, block, by):
        return source[c, pl.ds(block[0] + by, block[1])]

    def weigh(c, block, t, east, west):
        fce[c, pl.ds(*block)] = 0.25 - 0.3125 * (shifted(psi, c, block, 1) - shifted(psi, c, block, -1))
        fcn[c, pl.ds(*block)] = 0.25 + 0.3125 * (east - west)

    stages = [field, field1, field2, field3]

    def stage(step, s, blocks, tiles):
        source, base = stages[s].at[step], field.at[step]
        target = stages[s + 1].at[step] if s < 3 else field.at[step + 1]

        def work(c, block, t, east, west):
            here = pl.ds(*block)
            up, down = shifted(source, c, block, 1), shifted(source, c, block, -1)
            change = fcn[c, here] * (up - down) + (0.5 * (west + down) - t) + fce[c, here] * (east - west)
            if s == 0:
                change = FINE_START * change
            target[c, here] = FINE_BETAS[s] * base[c, here] + change

        over_tiles(source, blocks, tiles, work)

    def blocks_of(first, last):
        count = max((last - first + 7) // 8, 1)
        return [(first + 8 * i, 8) for i in range(count - 1)] + [(max(last - 8, first), 8)]

    def by_runs(work):
        def run(at, carry):
            work([at * SPAN + i for i in range(SPAN)])
            return carry

        lax.fori_loop(0, FT // SPAN, run, 0)

    untile(xwin, field.at[0], own)
    by_runs(lambda tiles: over_tiles(psi, blocks_of(HALO + 1, HALO + BAND - 1), tiles, weigh))
    for k in range(STAGES - 1):
        inner = blocks_of(HALO + k + 1, HALO + BAND - k - 1)
        by_runs(lambda tiles: stage(k // 4, k % 4, inner, tiles))

    for halo in halos[:2]:
        halo.wait_recv()
    untile(swin, psi, around)
    over_tiles(psi, [(1, HALO), (WIDE - 1 - HALO, HALO)], range(FT), weigh)
    restricted_window(psi, cpsi)
    middle_rows = [(1, 8), (7, 8)]
    for c in range(CT):
        for block in middle_rows:
            t = [cpsi[(c + d) % CT, pl.ds(*block)] for d in (-1, 0, 1)]
            west = jnp.where(first_lane(t[1]), pltpu.roll(t[0], 1, 1), pltpu.roll(t[1], 1, 1))
            east = jnp.where(last_lane(t[1]), pltpu.roll(t[2], LANES - 1, 1), pltpu.roll(t[1], LANES - 1, 1))
            cce[c, pl.ds(*block)] = 0.25 - 0.3125 * (shifted(cpsi, c, block, 1) - shifted(cpsi, c, block, -1))
            ccn[c, pl.ds(*block)] = 0.25 + 0.3125 * (east - west)

    for halo in halos[2:]:
        halo.wait_recv()
    untile(xwin, field.at[0], around)

    restricted_window(field.at[0], cfield.at[0])
    for s in range(4):
        for c in range(CT):
            for block in [(s + 1, 8), (7 - s, 8)][:2 if s < 3 else 1]:
                here = pl.ds(*block)
                t = [cfield[s, (c + d) % CT, here] for d in (-1, 0, 1)]
                west = jnp.where(first_lane(t[1]), pltpu.roll(t[0], 1, 1), pltpu.roll(t[1], 1, 1))
                east = jnp.where(last_lane(t[1]), pltpu.roll(t[2], LANES - 1, 1), pltpu.roll(t[1], LANES - 1, 1))
                up, down = shifted(cfield.at[s], c, block, 1), shifted(cfield.at[s], c, block, -1)
                change = ccn[c, here] * (up - down) + (0.5 * (west + down) - t[1]) + cce[c, here] * (east - west)
                if s == 0:
                    change = COARSE_START * change
                cfield[s + 1, c, here] = COARSE_BETAS[s] * cfield[0, c, here] + change
    coarse_old = [cfield.at[4, c, pl.ds(4, CROWS)] for c in range(CT)]

    def fine_step(step, carry):
        for s in range(4):
            done = 4 * step + s
            blocks = [(done + 1, HALO), (WIDE - HALO - 1 - done, HALO)]
            stage(step, s, blocks, range(FT))
        return carry

    lax.fori_loop(0, FINE_STEPS, fine_step, 0)
    fine_end = field.at[FINE_STEPS]

    ended = restricted_band(fine_end)
    gap = [ended[c] - coarse_old[c][...] for c in range(CT)]
    windows([jnp.where(n == 0, coarse_old[c][...] + gap[c], gap[c]) for c in range(CT)], wgap)

    middle = pl.ds(CROWS * REACH, CROWS)

    def gap_copy(k, m):
        return pltpu.make_async_remote_copy(
            src_ref=wgap.at[flipped(k, side)],
            dst_ref=pay.at[m, middle],
            send_sem=a_send.at[k],
            recv_sem=a_recv.at[m],
            device_id=(k, b),
            device_id_type=MESH,
        )

    for k in range(SLICES):
        @pl.when((n != k) & (n < SLICES - 1))
        def _():
            gap_copy(k, n).start()

    @pl.when(n < SLICES - 1)
    def _():
        pay[n, middle] = wgap[column]

    for spread in spreads:
        spread.wait()
    around_psi = jnp.stack([spw[pl.ds(4 + r, 8, stride=8)] for r in range(8)])
    ce, cn = coefficients(
        around_psi, pltpu.roll(around_psi, LANES - 1, 2), pltpu.roll(around_psi, 1, 2)
    )
    chain_weights = (ce, 0.5 - ce, cn, 0.5 - cn)

    for m in range(SLICES - 1):
        @pl.when(n != m)
        def _():
            gap_copy(m, m).wait_recv()

    gathers = []
    for at, j in enumerate(offsets):
        count = SLICES + 1 - 2 * abs(j)
        gathers.append(
            pltpu.make_async_remote_copy(
                src_ref=pay.at[pl.ds(0, count), middle],
                dst_ref=pay.at[pl.ds(0, count), pl.ds(CROWS * (REACH - j), CROWS)],
                send_sem=b_send.at[at],
                recv_sem=b_recv.at[at],
                device_id=at_window(j),
                device_id_type=MESH,
            )
        )
        gathers[-1].start()

    for gather in gathers:
        gather.wait_recv()

    def new_copy(i, window):
        return pltpu.make_async_remote_copy(
            src_ref=nbuf.at[i, middle],
            dst_ref=newc.at[window],
            send_sem=c_send.at[i],
            recv_sem=c_recv.at[window],
            device_id=(i, b),
            device_id_type=MESH,
        )

    def link(i, current):
        t = current
        for s in range(4):
            change = operator(t, pltpu.roll(t, LANES - 1, 2), pltpu.roll(t, 1, 2), *chain_weights)
            if s == 0:
                change = COARSE_START * change
            t = COARSE_BETAS[s] * current + change
        for r in range(8):
            nbuf[i, pl.ds(4 + r, 8, stride=8)] = t[r]

        @pl.when(i != n)
        def _():
            new_copy(i, column).start()

        @pl.when(i == n)
        def _():
            newc[column] = nbuf[i, middle]

        late = lax.rem(i, SLICES - 1)
        return t + jnp.stack([pay[late, pl.ds(4 + r, 8, stride=8)] for r in range(8)])

    first = jnp.stack([pay[0, pl.ds(4 + r, 8, stride=8)] for r in range(8)])
    lax.fori_loop(1, SLICES, link, first)

    for k in range(SLICES):
        @pl.when((n != k) & (n > 0))
        def _():
            new_copy(k, flipped(k, side)).wait_recv()

    lane = lax.broadcasted_iota(jnp.int32, (CROWS, LANES), 1)
    for c in range(CT):
        new = jnp.where(
            lane < LANES // 2, pltpu.roll(newc[2 * c], LANES - 32, 1), pltpu.roll(newc[2 * c + 1], 32, 1)
        )
        was = coarse_old[c][...]
        change = jnp.where(n == 0, was, new) - was
        for i in range(4):
            spread_rows[pl.ds(BAND * c + i, CROWS, stride=4)] = change
    fine_change = matmul(spread_rows[...], grow[...])
    for c in range(CT):
        for m in range(4):
            for i in range(BAND // 8):
                out[i, 4 * c + m] = (
                    fine_end[4 * c + m, pl.ds(HALO + 8 * i, 8)]
                    + fine_change[BAND * c + 8 * i:BAND * c + 8 * (i + 1), m * LANES:(m + 1) * LANES]
                )

    for halo in halos:
        halo.wait_send()
    for k in range(SLICES):
        @pl.when((n != k) & (n < SLICES - 1))
        def _():
            gap_copy(k, n).wait_send()
    for gather in gathers:
        gather.wait_send()
    for i in range(1, SLICES):
        @pl.when(n != i)
        def _():
            new_copy(i, column).wait_send()


def per_device(states, stream):
    fine = pltpu.VMEM((FT, WIDE, LANES), F32)
    by_step = pltpu.VMEM((FINE_STEPS, FT, WIDE, LANES), F32)
    coarse = pltpu.VMEM((CT, 2 * CROWS, LANES), F32)

    def tiled(x):
        return x.reshape(BAND // 8, 8, FT, LANES).transpose(0, 2, 1, 3)

    ended = pl.pallas_call(
        kernel,
        out_shape=pltpu.VMEM((BAND // 8, FT, 8, LANES), F32),
        in_specs=[pl.BlockSpec(memory_space=pl.ANY)] * 2,
        out_specs=pl.BlockSpec(memory_space=pltpu.VMEM),
        scratch_shapes=[
            pltpu.VMEM((WIDE // 8, FT, 8, LANES), F32),
            pltpu.VMEM((WIDE // 8, FT, 8, LANES), F32),
            fine,
            pltpu.VMEM((FINE_STEPS + 1, FT, WIDE, LANES), F32),
            by_step, by_step, by_step,
            fine,
            fine,
            pltpu.VMEM((4 * LANES, LANES), jnp.bfloat16),
            pltpu.VMEM((LANES, 4 * LANES), jnp.bfloat16),
            pltpu.VMEM((2 * CT * 8, 4 * LANES), F32),
            coarse,
            coarse,
            coarse,
            pltpu.VMEM((5, CT, 2 * CROWS, LANES), F32),
            pltpu.VMEM((SLICES, CROWS, LANES), F32),
            pltpu.VMEM((SLICES, CROWS, LANES), F32),
            pltpu.VMEM((CWIDE, LANES), F32),
            pltpu.VMEM((SLICES - 1, CWIDE, LANES), F32),
            pltpu.VMEM((SLICES, CWIDE, LANES), F32),
            pltpu.VMEM((SLICES, CROWS, LANES), F32),
            pltpu.VMEM((CT * BAND, LANES), F32),
            pltpu.SemaphoreType.DMA((2,)),
            pltpu.SemaphoreType.DMA((4,)),
            pltpu.SemaphoreType.DMA((4,)),
            pltpu.SemaphoreType.DMA((2 * REACH,)),
            pltpu.SemaphoreType.DMA((2 * REACH,)),
            pltpu.SemaphoreType.DMA((SLICES,)),
            pltpu.SemaphoreType.DMA((SLICES,)),
            pltpu.SemaphoreType.DMA((2 * REACH,)),
            pltpu.SemaphoreType.DMA((2 * REACH,)),
            pltpu.SemaphoreType.DMA((SLICES,)),
            pltpu.SemaphoreType.DMA((SLICES,)),
        ],
        compiler_params=pltpu.CompilerParams(
            collective_id=0, has_side_effects=True, vmem_limit_bytes=60 * 1024 * 1024
        ),
    )(tiled(states), tiled(stream))
    return ended.transpose(0, 2, 1, 3).reshape(1, BAND, COLS)


def solution(mesh):
    in_specs = (P("cuts", "space", None), P("space", None))
    out_specs = P("cuts", "space", None)
    return jax.shard_map(
        per_device, mesh=mesh, in_specs=in_specs, out_specs=out_specs, check_vma=False
    )
```

```python
import jax
import jax.numpy as jnp
from jax import lax
from jax.experimental import pallas as pl
from jax.experimental.pallas import tpu as pltpu
from jax.sharding import PartitionSpec as P

MESH = pl.DeviceIdType.MESH
LANES = 128
COLS = 2048
FT = COLS // LANES
CT = FT // 4
BAND = 32
HALO = 16
WIDE = BAND + 2 * HALO
SLICES = 8
SPACE = 16
REACH = 4
CROWS = 8
CWIDE = CROWS * (2 * REACH + 1)
FINE_STEPS = 4
SPAN = 4
STAGES = 4 * FINE_STEPS
F32 = jnp.float32


def scales(step, kappa):
    gains = [step / (4 - s) / kappa for s in range(4)]
    betas = [1.0] * 4
    for s in (2, 1, 0):
        betas[s] = betas[s + 1] * gains[s + 1]
    return betas, betas[0] * gains[0]


FINE_BETAS, FINE_START = scales(0.25, 1.25)
COARSE_BETAS, COARSE_START = scales(1.0, 20.0)


def rows_up(t):
    return jnp.concatenate([t[1:], pltpu.roll(t[:1], 7, 1)], axis=0)


def rows_down(t):
    return jnp.concatenate([pltpu.roll(t[-1:], 1, 1), t[:-1]], axis=0)


def coefficients(psi, east, west):
    ce = 0.25 - 0.3125 * (rows_up(psi) - rows_down(psi))
    cn = 0.25 + 0.3125 * (east - west)
    return ce, cn


def operator(t, east, west, ce, cw, cn, cs):
    return ce * east + cw * west + cn * rows_up(t) + cs * rows_down(t) - t


def matmul(x, m):
    high = x.astype(jnp.bfloat16)
    x = x - high.astype(F32)
    middle = x.astype(jnp.bfloat16)
    low = (x - middle.astype(F32)).astype(jnp.bfloat16)
    small = jnp.dot(low, m, preferred_element_type=F32) + jnp.dot(middle, m, preferred_element_type=F32)
    return jnp.dot(high, m, preferred_element_type=F32) + small


def kernel(
    states, stream, out,
    xwin, swin, psi, field, field1, field2, field3, fce, fcn, shrink, grow, rows, cpsi, cce, ccn, cfield, wstream, wgap, spw, pay, nbuf, newc, spread_rows,
    local_sem, halo_send, halo_recv, sc_send, sc_recv, a_send, a_recv, b_send, b_recv, c_send, c_recv,
):
    n = lax.axis_index("cuts")
    b = lax.axis_index("space")

    def flipped(k, bit):
        return k + bit * (1 - 2 * lax.rem(k, 2))

    side = lax.rem(b // 2, 2)
    column = flipped(n, side)

    def at_space(j):
        return (n, lax.rem(b + (SPACE + j), SPACE))

    def at_window(j):
        other = lax.rem(b + (SPACE + j), SPACE)
        return (flipped(n, lax.rem(side + lax.rem(other // 2, 2), 2)), other)

    across = 2 * lax.rem(b, 2) - 1
    offsets = [(1, across)] + [(d, j) for d in range(2, REACH + 1) for j in (-d, d)] + [(1, -across)]
    others = [lax.rem(n + k, SLICES) for k in (4, 5, 3, 2, 6, 1, 7)]


    own_x = pltpu.make_async_copy(states, xwin.at[pl.ds(HALO // 8, BAND // 8)], local_sem.at[0])
    own_s = pltpu.make_async_copy(stream, swin.at[pl.ds(HALO // 8, BAND // 8)], local_sem.at[1])
    own_s.start()
    own_x.start()

    pay[...] = jnp.zeros_like(pay)
    newc[...] = jnp.zeros_like(newc)

    barrier = pltpu.get_barrier_semaphore()
    greeted = [at_space(across)]
    greeted += [(k, b) for k in others]
    greeted += [at_window(j) for _, j in offsets]
    for device in greeted:
        pl.semaphore_signal(barrier, inc=1, device_id=device, device_id_type=MESH)
    pl.semaphore_wait(barrier, len(greeted))

    halos = []
    for at, (source, window, device) in enumerate(((stream, swin, at_space), (states, xwin, at_space))):
        for end, (j, first, target) in enumerate(((1, BAND - HALO, 0), (-1, 0, HALO + BAND))):
            halos.append(
                pltpu.make_async_remote_copy(
                    src_ref=source.at[pl.ds(first // 8, HALO // 8)],
                    dst_ref=window.at[pl.ds(target // 8, HALO // 8)],
                    send_sem=halo_send.at[2 * at + end],
                    recv_sem=halo_recv.at[2 * at + end],
                    device_id=device(j),
                    device_id_type=MESH,
                )
            )
            halos[-1].start()

    fine_at = lax.broadcasted_iota(jnp.int32, (4 * LANES, LANES), 0)
    coarse_at = lax.broadcasted_iota(jnp.int32, (4 * LANES, LANES), 1)
    shrink[...] = jnp.where((fine_at >> 2) == coarse_at, 0.0625, 0.0).astype(jnp.bfloat16)
    fine_at = lax.broadcasted_iota(jnp.int32, (LANES, 4 * LANES), 1)
    coarse_at = lax.broadcasted_iota(jnp.int32, (LANES, 4 * LANES), 0)
    grow[...] = jnp.where((fine_at >> 2) == coarse_at, 1.0, 0.0).astype(jnp.bfloat16)

    def windows(tiles, target):
        lane = lax.broadcasted_iota(jnp.int32, (CROWS, LANES), 1)
        right = [pltpu.roll(t, 32, 1) for t in tiles]
        left = [pltpu.roll(t, LANES - 32, 1) for t in tiles]
        for j in range(CT):
            target[2 * j] = jnp.where(lane < 32, right[(j - 1) % CT], right[j])
            target[2 * j + 1] = jnp.where(lane < LANES - 32, left[j], left[(j + 1) % CT])

    own = range(HALO // 8, (HALO + BAND) // 8)
    around = [i for i in range(WIDE // 8) if i not in own]

    def untile(window, target, parts):
        for i in parts:
            for c in range(FT):
                target[c, pl.ds(8 * i, 8)] = window[i, c]

    def add_rows(source, at, first):
        for c in range(FT):
            parts = [source[c, pl.ds(first + i, 8, stride=4)] for i in range(4)]
            rows[pl.ds(at(c // 4), 8), pl.ds(c % 4 * LANES, LANES)] = parts[0] + parts[1] + (parts[2] + parts[3])

    def restricted_band(source):
        add_rows(source, lambda c: CROWS * c, HALO)
        small = matmul(rows[pl.ds(0, CROWS * CT)], shrink[...])
        return [small[CROWS * c:CROWS * (c + 1)] for c in range(CT)]

    def restricted_window(source, target):
        for half in range(2):
            add_rows(source, lambda c: 2 * CROWS * c + CROWS * half, half * WIDE // 2)
        small = matmul(rows[...], shrink[...])
        for c in range(CT):
            target[c] = small[2 * CROWS * c:2 * CROWS * (c + 1)]

    own_s.wait()
    untile(swin, psi, own)
    windows(restricted_band(psi), wstream)
    spreads = []
    for at, (_, j) in enumerate(offsets):
        spreads.append(
            pltpu.make_async_remote_copy(
                src_ref=wstream.at[column],
                dst_ref=spw.at[pl.ds(pl.multiple_of(CROWS * (REACH - j), CROWS), CROWS)],
                send_sem=sc_send.at[at],
                recv_sem=sc_recv.at[at],
                device_id=at_window(j),
                device_id_type=MESH,
            )
        )
        spreads[-1].start()
    spw[pl.ds(CROWS * REACH, CROWS)] = wstream[column]
    own_x.wait()

    def first_lane(t):
        return lax.broadcasted_iota(jnp.int32, t.shape, 1) == 0

    def last_lane(t):
        return lax.broadcasted_iota(jnp.int32, t.shape, 1) == LANES - 1

    def wrapped(c):
        return c % FT if isinstance(c, int) else lax.rem(c, FT)

    def over_tiles(source, blocks, tiles, work):
        def west_of(c):
            return [pltpu.roll(source[c, pl.ds(*block)], 1, 1) for block in blocks]

        def east_of(c):
            return [pltpu.roll(source[c, pl.ds(*block)], LANES - 1, 1) for block in blocks]

        before, now = west_of(wrapped(tiles[0] + FT - 1)), east_of(tiles[0])
        for c in tiles:
            west_now, after = west_of(c), east_of(wrapped(c + 1))
            for i, block in enumerate(blocks):
                t = source[c, pl.ds(*block)]
                west = jnp.where(first_lane(t), before[i], west_now[i])
                east = jnp.where(last_lane(t), after[i], now[i])
                work(c, block, t, east, west)
            before, now = west_now, after

    def shifted(source, c, block, by):
        return source[c, pl.ds(block[0] + by, block[1])]

    def weigh(c, block, t, east, west):
        fce[c, pl.ds(*block)] = 0.25 - 0.3125 * (shifted(psi, c, block, 1) - shifted(psi, c, block, -1))
        fcn[c, pl.ds(*block)] = 0.25 + 0.3125 * (east - west)

    stages = [field, field1, field2, field3]

    def stage(step, s, blocks, tiles):
        source, base = stages[s].at[step], field.at[step]
        target = stages[s + 1].at[step] if s < 3 else field.at[step + 1]

        def work(c, block, t, east, west):
            here = pl.ds(*block)
            up, down = shifted(source, c, block, 1), shifted(source, c, block, -1)
            change = fcn[c, here] * (up - down) + (0.5 * (west + down) - t) + fce[c, here] * (east - west)
            if s == 0:
                change = FINE_START * change
            target[c, here] = FINE_BETAS[s] * base[c, here] + change

        over_tiles(source, blocks, tiles, work)

    def blocks_of(first, last):
        count = max((last - first + 7) // 8, 1)
        return [(first + 8 * i, 8) for i in range(count - 1)] + [(max(last - 8, first), 8)]

    def by_runs(work):
        def run(at, carry):
            work([at * SPAN + i for i in range(SPAN)])
            return carry

        lax.fori_loop(0, FT // SPAN, run, 0)

    untile(xwin, field.at[0], own)
    by_runs(lambda tiles: over_tiles(psi, blocks_of(HALO + 1, HALO + BAND - 1), tiles, weigh))
    for k in range(STAGES - 1):
        inner = blocks_of(HALO + k + 1, HALO + BAND - k - 1)
        by_runs(lambda tiles: stage(k // 4, k % 4, inner, tiles))

    for halo in halos[:2]:
        halo.wait_recv()
    untile(swin, psi, around)
    over_tiles(psi, [(1, HALO), (WIDE - 1 - HALO, HALO)], range(FT), weigh)
    restricted_window(psi, cpsi)
    middle_rows = [(1, 8), (7, 8)]
    for c in range(CT):
        for block in middle_rows:
            t = [cpsi[(c + d) % CT, pl.ds(*block)] for d in (-1, 0, 1)]
            west = jnp.where(first_lane(t[1]), pltpu.roll(t[0], 1, 1), pltpu.roll(t[1], 1, 1))
            east = jnp.where(last_lane(t[1]), pltpu.roll(t[2], LANES - 1, 1), pltpu.roll(t[1], LANES - 1, 1))
            cce[c, pl.ds(*block)] = 0.25 - 0.3125 * (shifted(cpsi, c, block, 1) - shifted(cpsi, c, block, -1))
            ccn[c, pl.ds(*block)] = 0.25 + 0.3125 * (east - west)

    for halo in halos[2:]:
        halo.wait_recv()
    untile(xwin, field.at[0], around)

    restricted_window(field.at[0], cfield.at[0])
    for s in range(4):
        for c in range(CT):
            for block in [(s + 1, 8), (7 - s, 8)][:2 if s < 3 else 1]:
                here = pl.ds(*block)
                t = [cfield[s, (c + d) % CT, here] for d in (-1, 0, 1)]
                west = jnp.where(first_lane(t[1]), pltpu.roll(t[0], 1, 1), pltpu.roll(t[1], 1, 1))
                east = jnp.where(last_lane(t[1]), pltpu.roll(t[2], LANES - 1, 1), pltpu.roll(t[1], LANES - 1, 1))
                up, down = shifted(cfield.at[s], c, block, 1), shifted(cfield.at[s], c, block, -1)
                change = ccn[c, here] * (up - down) + (0.5 * (west + down) - t[1]) + cce[c, here] * (east - west)
                if s == 0:
                    change = COARSE_START * change
                cfield[s + 1, c, here] = COARSE_BETAS[s] * cfield[0, c, here] + change
    coarse_old = [cfield.at[4, c, pl.ds(4, CROWS)] for c in range(CT)]

    def fine_step(step, carry):
        for s in range(4):
            done = 4 * step + s
            blocks = [(done + 1, HALO), (WIDE - HALO - 1 - done, HALO)]
            stage(step, s, blocks, [(c + s) % FT for c in range(FT)])
        return carry

    lax.fori_loop(0, FINE_STEPS, fine_step, 0)
    fine_end = field.at[FINE_STEPS]

    ended = restricted_band(fine_end)
    gap = [ended[c] - coarse_old[c][...] for c in range(CT)]
    windows([jnp.where(n == 0, coarse_old[c][...] + gap[c], gap[c]) for c in range(CT)], wgap)

    middle = pl.ds(CROWS * REACH, CROWS)

    def gap_copy(k, m):
        return pltpu.make_async_remote_copy(
            src_ref=wgap.at[flipped(k, side)],
            dst_ref=pay.at[m, middle],
            send_sem=a_send.at[k],
            recv_sem=a_recv.at[m],
            device_id=(k, b),
            device_id_type=MESH,
        )

    @pl.when(n < SLICES - 1)
    def _():
        for k in others:
            gap_copy(k, n).start()
        pay[n, middle] = wgap[column]

    for spread in spreads:
        spread.wait()
    around_psi = jnp.stack([spw[pl.ds(4 + r, 8, stride=8)] for r in range(8)])
    ce, cn = coefficients(
        around_psi, pltpu.roll(around_psi, LANES - 1, 2), pltpu.roll(around_psi, 1, 2)
    )
    chain_weights = (ce, 0.5 - ce, cn, 0.5 - cn)

    for m in range(SLICES - 1):
        @pl.when(n != m)
        def _():
            gap_copy(m, m).wait_recv()

    gathers = []
    for at, (distance, j) in enumerate(offsets):
        count = SLICES + 1 - 2 * distance
        gathers.append(
            pltpu.make_async_remote_copy(
                src_ref=pay.at[pl.ds(0, count), middle],
                dst_ref=pay.at[pl.ds(0, count), pl.ds(pl.multiple_of(CROWS * (REACH - j), CROWS), CROWS)],
                send_sem=b_send.at[at],
                recv_sem=b_recv.at[at],
                device_id=at_window(j),
                device_id_type=MESH,
            )
        )
        gathers[-1].start()

    for halo in halos:
        halo.wait_send()

    @pl.when(n < SLICES - 1)
    def _():
        for k in others:
            gap_copy(k, n).wait_send()

    for gather in gathers:
        gather.wait_recv()

    def new_copy(i, window):
        return pltpu.make_async_remote_copy(
            src_ref=nbuf.at[i, middle],
            dst_ref=newc.at[window],
            send_sem=c_send.at[i],
            recv_sem=c_recv.at[window],
            device_id=(i, b),
            device_id_type=MESH,
        )

    def link(i, current):
        t = current
        for s in range(4):
            change = operator(t, pltpu.roll(t, LANES - 1, 2), pltpu.roll(t, 1, 2), *chain_weights)
            if s == 0:
                change = COARSE_START * change
            t = COARSE_BETAS[s] * current + change
        for r in range(8):
            nbuf[i, pl.ds(4 + r, 8, stride=8)] = t[r]

        @pl.when(i != n)
        def _():
            new_copy(i, column).start()

        @pl.when(i == n)
        def _():
            newc[column] = nbuf[i, middle]

        late = lax.rem(i, SLICES - 1)
        return t + jnp.stack([pay[late, pl.ds(4 + r, 8, stride=8)] for r in range(8)])

    first = jnp.stack([pay[0, pl.ds(4 + r, 8, stride=8)] for r in range(8)])
    lax.fori_loop(1, SLICES, link, first)

    for gather in gathers:
        gather.wait_send()
    for i in range(1, SLICES):
        @pl.when(n != i)
        def _():
            new_copy(i, column).wait_send()

    for k in range(SLICES):
        @pl.when((n != k) & (n > 0))
        def _():
            new_copy(k, flipped(k, side)).wait_recv()

    lane = lax.broadcasted_iota(jnp.int32, (CROWS, LANES), 1)
    for c in range(CT):
        new = jnp.where(
            lane < LANES // 2, pltpu.roll(newc[2 * c], LANES - 32, 1), pltpu.roll(newc[2 * c + 1], 32, 1)
        )
        was = coarse_old[c][...]
        change = jnp.where(n == 0, was, new) - was
        for i in range(4):
            spread_rows[pl.ds(BAND * c + i, CROWS, stride=4)] = change
    fine_change = matmul(spread_rows[...], grow[...])
    for c in range(CT):
        for m in range(4):
            for i in range(BAND // 8):
                out[i, 4 * c + m] = (
                    fine_end[4 * c + m, pl.ds(HALO + 8 * i, 8)]
                    + fine_change[BAND * c + 8 * i:BAND * c + 8 * (i + 1), m * LANES:(m + 1) * LANES]
                )


def per_device(states, stream):
    fine = pltpu.VMEM((FT, WIDE, LANES), F32)
    by_step = pltpu.VMEM((FINE_STEPS, FT, WIDE, LANES), F32)
    coarse = pltpu.VMEM((CT, 2 * CROWS, LANES), F32)

    def tiled(x):
        return x.reshape(BAND // 8, 8, FT, LANES).transpose(0, 2, 1, 3)

    ended = pl.pallas_call(
        kernel,
        out_shape=pltpu.VMEM((BAND // 8, FT, 8, LANES), F32),
        in_specs=[pl.BlockSpec(memory_space=pl.ANY)] * 2,
        out_specs=pl.BlockSpec(memory_space=pltpu.VMEM),
        scratch_shapes=[
            pltpu.VMEM((WIDE // 8, FT, 8, LANES), F32),
            pltpu.VMEM((WIDE // 8, FT, 8, LANES), F32),
            fine,
            pltpu.VMEM((FINE_STEPS + 1, FT, WIDE, LANES), F32),
            by_step, by_step, by_step,
            fine,
            fine,
            pltpu.VMEM((4 * LANES, LANES), jnp.bfloat16),
            pltpu.VMEM((LANES, 4 * LANES), jnp.bfloat16),
            pltpu.VMEM((2 * CT * 8, 4 * LANES), F32),
            coarse,
            coarse,
            coarse,
            pltpu.VMEM((5, CT, 2 * CROWS, LANES), F32),
            pltpu.VMEM((SLICES, CROWS, LANES), F32),
            pltpu.VMEM((SLICES, CROWS, LANES), F32),
            pltpu.VMEM((CWIDE, LANES), F32),
            pltpu.VMEM((SLICES - 1, CWIDE, LANES), F32),
            pltpu.VMEM((SLICES, CWIDE, LANES), F32),
            pltpu.VMEM((SLICES, CROWS, LANES), F32),
            pltpu.VMEM((CT * BAND, LANES), F32),
            pltpu.SemaphoreType.DMA((2,)),
            pltpu.SemaphoreType.DMA((4,)),
            pltpu.SemaphoreType.DMA((4,)),
            pltpu.SemaphoreType.DMA((2 * REACH,)),
            pltpu.SemaphoreType.DMA((2 * REACH,)),
            pltpu.SemaphoreType.DMA((SLICES,)),
            pltpu.SemaphoreType.DMA((SLICES,)),
            pltpu.SemaphoreType.DMA((2 * REACH,)),
            pltpu.SemaphoreType.DMA((2 * REACH,)),
            pltpu.SemaphoreType.DMA((SLICES,)),
            pltpu.SemaphoreType.DMA((SLICES,)),
        ],
        compiler_params=pltpu.CompilerParams(
            collective_id=0, has_side_effects=True, vmem_limit_bytes=60 * 1024 * 1024
        ),
    )(tiled(states), tiled(stream))
    return ended.transpose(0, 2, 1, 3).reshape(1, BAND, COLS)


def solution(mesh):
    in_specs = (P("cuts", "space", None), P("space", None))
    out_specs = P("cuts", "space", None)
    return jax.shard_map(
        per_device, mesh=mesh, in_specs=in_specs, out_specs=out_specs, check_vma=False
    )
```

```python
import jax
import jax.numpy as jnp
from jax import lax
from jax.experimental import pallas as pl
from jax.experimental.pallas import tpu as pltpu
from jax.sharding import PartitionSpec as P

MESH = pl.DeviceIdType.MESH
LANES = 128
COLS = 2048
FT = COLS // LANES
CT = FT // 4
BAND = 32
HALO = 16
WIDE = BAND + 2 * HALO
SLICES = 8
SPACE = 16
REACH = 4
CROWS = 8
CWIDE = CROWS * (2 * REACH + 1)
FINE_STEPS = 4
SPAN = 4
STAGES = 4 * FINE_STEPS
F32 = jnp.float32


def scales(step, kappa):
    gains = [step / (4 - s) / kappa for s in range(4)]
    betas = [1.0] * 4
    for s in (2, 1, 0):
        betas[s] = betas[s + 1] * gains[s + 1]
    return betas, betas[0] * gains[0]


FINE_BETAS, FINE_START = scales(0.25, 1.25)
COARSE_BETAS, COARSE_START = scales(1.0, 20.0)


def rows_up(t):
    return jnp.concatenate([t[1:], pltpu.roll(t[:1], 7, 1)], axis=0)


def rows_down(t):
    return jnp.concatenate([pltpu.roll(t[-1:], 1, 1), t[:-1]], axis=0)


def coefficients(psi, east, west):
    ce = 0.25 - 0.3125 * (rows_up(psi) - rows_down(psi))
    cn = 0.25 + 0.3125 * (east - west)
    return ce, cn


def operator(t, east, west, ce, cw, cn, cs):
    return ce * east + cw * west + cn * rows_up(t) + cs * rows_down(t) - t


def matmul(x, m):
    high = x.astype(jnp.bfloat16)
    x = x - high.astype(F32)
    middle = x.astype(jnp.bfloat16)
    low = (x - middle.astype(F32)).astype(jnp.bfloat16)
    small = jnp.dot(low, m, preferred_element_type=F32) + jnp.dot(middle, m, preferred_element_type=F32)
    return jnp.dot(high, m, preferred_element_type=F32) + small


def kernel(
    states, stream, out,
    xwin, swin, psi, field, field1, field2, field3, fce, fcn, shrink, grow, rows, cpsi, cce, ccn, cfield, wstream, wgap, spw, pay, nbuf, newc, spread_rows,
    local_sem, halo_send, halo_recv, sc_send, sc_recv, a_send, a_recv, b_send, b_recv, c_send, c_recv,
):
    n = lax.axis_index("cuts")
    b = lax.axis_index("space")

    def flipped(k, bit):
        return k + bit * (1 - 2 * lax.rem(k, 2))

    side = lax.rem(b // 2, 2)
    column = flipped(n, side)

    def at_space(j):
        return (n, lax.rem(b + (SPACE + j), SPACE))

    def at_window(j):
        other = lax.rem(b + (SPACE + j), SPACE)
        return (flipped(n, lax.rem(side + lax.rem(other // 2, 2), 2)), other)

    across = 2 * lax.rem(b, 2) - 1
    offsets = [(1, across)] + [(d, j) for d in range(2, REACH + 1) for j in (-d, d)] + [(1, -across)]
    others = [lax.rem(n + k, SLICES) for k in (4, 5, 3, 2, 6, 1, 7)]


    own_x = pltpu.make_async_copy(states, xwin.at[pl.ds(HALO // 8, BAND // 8)], local_sem.at[0])
    own_s = pltpu.make_async_copy(stream, swin.at[pl.ds(HALO // 8, BAND // 8)], local_sem.at[1])
    own_s.start()
    own_x.start()

    pay[...] = jnp.zeros_like(pay)
    newc[...] = jnp.zeros_like(newc)

    barrier = pltpu.get_barrier_semaphore()
    greeted = [at_space(across)]
    greeted += [(k, b) for k in others]
    greeted += [at_window(j) for _, j in offsets]
    for device in greeted:
        pl.semaphore_signal(barrier, inc=1, device_id=device, device_id_type=MESH)
    pl.semaphore_wait(barrier, len(greeted))

    halos = []
    for at, (source, window, device) in enumerate(((stream, swin, at_space), (states, xwin, at_space))):
        for end, (j, first, target) in enumerate(((1, BAND - HALO, 0), (-1, 0, HALO + BAND))):
            halos.append(
                pltpu.make_async_remote_copy(
                    src_ref=source.at[pl.ds(first // 8, HALO // 8)],
                    dst_ref=window.at[pl.ds(target // 8, HALO // 8)],
                    send_sem=halo_send.at[2 * at + end],
                    recv_sem=halo_recv.at[2 * at + end],
                    device_id=device(j),
                    device_id_type=MESH,
                )
            )
            halos[-1].start()

    fine_at = lax.broadcasted_iota(jnp.int32, (4 * LANES, LANES), 0)
    coarse_at = lax.broadcasted_iota(jnp.int32, (4 * LANES, LANES), 1)
    shrink[...] = jnp.where((fine_at >> 2) == coarse_at, 0.0625, 0.0).astype(jnp.bfloat16)
    fine_at = lax.broadcasted_iota(jnp.int32, (LANES, 4 * LANES), 1)
    coarse_at = lax.broadcasted_iota(jnp.int32, (LANES, 4 * LANES), 0)
    grow[...] = jnp.where((fine_at >> 2) == coarse_at, 1.0, 0.0).astype(jnp.bfloat16)

    def windows(tiles, target):
        lane = lax.broadcasted_iota(jnp.int32, (CROWS, LANES), 1)
        right = [pltpu.roll(t, 32, 1) for t in tiles]
        left = [pltpu.roll(t, LANES - 32, 1) for t in tiles]
        for j in range(CT):
            target[2 * j] = jnp.where(lane < 32, right[(j - 1) % CT], right[j])
            target[2 * j + 1] = jnp.where(lane < LANES - 32, left[j], left[(j + 1) % CT])

    own = range(HALO // 8, (HALO + BAND) // 8)
    around = [i for i in range(WIDE // 8) if i not in own]

    def untile(window, target, parts):
        for i in parts:
            for c in range(FT):
                target[c, pl.ds(8 * i, 8)] = window[i, c]

    def add_rows(source, at, first):
        for c in range(FT):
            parts = [source[c, pl.ds(first + i, 8, stride=4)] for i in range(4)]
            rows[pl.ds(at(c // 4), 8), pl.ds(c % 4 * LANES, LANES)] = parts[0] + parts[1] + (parts[2] + parts[3])

    def restricted_band(source):
        add_rows(source, lambda c: CROWS * c, HALO)
        small = matmul(rows[pl.ds(0, CROWS * CT)], shrink[...])
        return [small[CROWS * c:CROWS * (c + 1)] for c in range(CT)]

    def restricted_window(source, target):
        for half in range(2):
            add_rows(source, lambda c: 2 * CROWS * c + CROWS * half, half * WIDE // 2)
        small = matmul(rows[...], shrink[...])
        for c in range(CT):
            target[c] = small[2 * CROWS * c:2 * CROWS * (c + 1)]

    own_s.wait()
    untile(swin, psi, own)
    windows(restricted_band(psi), wstream)
    spreads = []
    for at, (_, j) in enumerate(offsets):
        spreads.append(
            pltpu.make_async_remote_copy(
                src_ref=wstream.at[column],
                dst_ref=spw.at[pl.ds(pl.multiple_of(CROWS * (REACH - j), CROWS), CROWS)],
                send_sem=sc_send.at[at],
                recv_sem=sc_recv.at[at],
                device_id=at_window(j),
                device_id_type=MESH,
            )
        )
        spreads[-1].start()
    spw[pl.ds(CROWS * REACH, CROWS)] = wstream[column]
    own_x.wait()

    def first_lane(t):
        return lax.broadcasted_iota(jnp.int32, t.shape, 1) == 0

    def last_lane(t):
        return lax.broadcasted_iota(jnp.int32, t.shape, 1) == LANES - 1

    def wrapped(c):
        return c % FT if isinstance(c, int) else lax.rem(c, FT)

    def over_tiles(source, blocks, tiles, work):
        def west_of(c):
            return [pltpu.roll(source[c, pl.ds(*block)], 1, 1) for block in blocks]

        def east_of(c):
            return [pltpu.roll(source[c, pl.ds(*block)], LANES - 1, 1) for block in blocks]

        before, now = west_of(wrapped(tiles[0] + FT - 1)), east_of(tiles[0])
        for c in tiles:
            west_now, after = west_of(c), east_of(wrapped(c + 1))
            for i, block in enumerate(blocks):
                t = source[c, pl.ds(*block)]
                west = jnp.where(first_lane(t), before[i], west_now[i])
                east = jnp.where(last_lane(t), after[i], now[i])
                work(c, block, t, east, west)
            before, now = west_now, after

    def shifted(source, c, block, by):
        return source[c, pl.ds(block[0] + by, block[1])]

    def weigh(c, block, t, east, west):
        fce[c, pl.ds(*block)] = 0.25 - 0.3125 * (shifted(psi, c, block, 1) - shifted(psi, c, block, -1))
        fcn[c, pl.ds(*block)] = 0.25 + 0.3125 * (east - west)

    stages = [field, field1, field2, field3]

    def stage(step, s, blocks, tiles):
        source, base = stages[s].at[step], field.at[step]
        target = stages[s + 1].at[step] if s < 3 else field.at[step + 1]

        def work(c, block, t, east, west):
            here = pl.ds(*block)
            up, down = shifted(source, c, block, 1), shifted(source, c, block, -1)
            change = fcn[c, here] * (up - down) + (0.5 * (west + down) - t) + fce[c, here] * (east - west)
            if s == 0:
                change = FINE_START * change
            target[c, here] = FINE_BETAS[s] * base[c, here] + change

        over_tiles(source, blocks, tiles, work)

    def blocks_of(first, last):
        count = max((last - first + 7) // 8, 1)
        return [(first + 8 * i, 8) for i in range(count - 1)] + [(max(last - 8, first), 8)]

    def by_runs(work):
        def run(at, carry):
            work([at * SPAN + i for i in range(SPAN)])
            return carry

        lax.fori_loop(0, FT // SPAN, run, 0)

    untile(xwin, field.at[0], own)
    by_runs(lambda tiles: over_tiles(psi, blocks_of(HALO + 1, HALO + BAND - 1), tiles, weigh))
    for k in range(STAGES - 1):
        inner = blocks_of(HALO + k + 1, HALO + BAND - k - 1)
        by_runs(lambda tiles: stage(k // 4, k % 4, inner, tiles))

    for halo in halos[:2]:
        halo.wait_recv()
    untile(swin, psi, around)
    over_tiles(psi, [(1, HALO), (WIDE - 1 - HALO, HALO)], range(FT), weigh)
    restricted_window(psi, cpsi)
    middle_rows = [(1, 8), (7, 8)]
    for c in range(CT):
        for block in middle_rows:
            t = [cpsi[(c + d) % CT, pl.ds(*block)] for d in (-1, 0, 1)]
            west = jnp.where(first_lane(t[1]), pltpu.roll(t[0], 1, 1), pltpu.roll(t[1], 1, 1))
            east = jnp.where(last_lane(t[1]), pltpu.roll(t[2], LANES - 1, 1), pltpu.roll(t[1], LANES - 1, 1))
            cce[c, pl.ds(*block)] = 0.25 - 0.3125 * (shifted(cpsi, c, block, 1) - shifted(cpsi, c, block, -1))
            ccn[c, pl.ds(*block)] = 0.25 + 0.3125 * (east - west)

    for halo in halos[2:]:
        halo.wait_recv()
    untile(xwin, field.at[0], around)

    restricted_window(field.at[0], cfield.at[0])
    for s in range(4):
        for c in range(CT):
            for block in [(s + 1, 8), (7 - s, 8)][:2 if s < 3 else 1]:
                here = pl.ds(*block)
                t = [cfield[s, (c + d) % CT, here] for d in (-1, 0, 1)]
                west = jnp.where(first_lane(t[1]), pltpu.roll(t[0], 1, 1), pltpu.roll(t[1], 1, 1))
                east = jnp.where(last_lane(t[1]), pltpu.roll(t[2], LANES - 1, 1), pltpu.roll(t[1], LANES - 1, 1))
                up, down = shifted(cfield.at[s], c, block, 1), shifted(cfield.at[s], c, block, -1)
                change = ccn[c, here] * (up - down) + (0.5 * (west + down) - t[1]) + cce[c, here] * (east - west)
                if s == 0:
                    change = COARSE_START * change
                cfield[s + 1, c, here] = COARSE_BETAS[s] * cfield[0, c, here] + change
    coarse_old = [cfield.at[4, c, pl.ds(4, CROWS)] for c in range(CT)]

    for step in range(FINE_STEPS):
        for s in range(4):
            done = 4 * step + s
            blocks = [(done + 1, HALO), (WIDE - HALO - 1 - done, HALO)]
            stage(step, s, blocks, [(c + s) % FT for c in range(FT)])
    fine_end = field.at[FINE_STEPS]

    ended = restricted_band(fine_end)
    gap = [ended[c] - coarse_old[c][...] for c in range(CT)]
    windows([jnp.where(n == 0, coarse_old[c][...] + gap[c], gap[c]) for c in range(CT)], wgap)

    middle = pl.ds(CROWS * REACH, CROWS)

    def gap_copy(k, m):
        return pltpu.make_async_remote_copy(
            src_ref=wgap.at[flipped(k, side)],
            dst_ref=pay.at[m, middle],
            send_sem=a_send.at[k],
            recv_sem=a_recv.at[m],
            device_id=(k, b),
            device_id_type=MESH,
        )

    @pl.when(n < SLICES - 1)
    def _():
        for k in others:
            gap_copy(k, n).start()
        pay[n, middle] = wgap[column]

    for spread in spreads:
        spread.wait()
    around_psi = jnp.stack([spw[pl.ds(4 + r, 8, stride=8)] for r in range(8)])
    ce, cn = coefficients(
        around_psi, pltpu.roll(around_psi, LANES - 1, 2), pltpu.roll(around_psi, 1, 2)
    )
    chain_weights = (ce, 0.5 - ce, cn, 0.5 - cn)

    for m in range(SLICES - 1):
        @pl.when(n != m)
        def _():
            gap_copy(m, m).wait_recv()

    gathers = []
    for at, (distance, j) in enumerate(offsets):
        count = SLICES + 1 - 2 * distance
        gathers.append(
            pltpu.make_async_remote_copy(
                src_ref=pay.at[pl.ds(0, count), middle],
                dst_ref=pay.at[pl.ds(0, count), pl.ds(pl.multiple_of(CROWS * (REACH - j), CROWS), CROWS)],
                send_sem=b_send.at[at],
                recv_sem=b_recv.at[at],
                device_id=at_window(j),
                device_id_type=MESH,
            )
        )
        gathers[-1].start()

    for halo in halos:
        halo.wait_send()

    @pl.when(n < SLICES - 1)
    def _():
        for k in others:
            gap_copy(k, n).wait_send()

    for gather in gathers:
        gather.wait_recv()

    def new_copy(i, window):
        return pltpu.make_async_remote_copy(
            src_ref=nbuf.at[i, middle],
            dst_ref=newc.at[window],
            send_sem=c_send.at[i],
            recv_sem=c_recv.at[window],
            device_id=(i, b),
            device_id_type=MESH,
        )

    def link(i, current):
        t = current
        for s in range(4):
            change = operator(t, pltpu.roll(t, LANES - 1, 2), pltpu.roll(t, 1, 2), *chain_weights)
            if s == 0:
                change = COARSE_START * change
            t = COARSE_BETAS[s] * current + change
        for r in range(8):
            nbuf[i, pl.ds(4 + r, 8, stride=8)] = t[r]

        @pl.when(i != n)
        def _():
            new_copy(i, column).start()

        @pl.when(i == n)
        def _():
            newc[column] = nbuf[i, middle]

        late = lax.rem(i, SLICES - 1)
        return t + jnp.stack([pay[late, pl.ds(4 + r, 8, stride=8)] for r in range(8)])

    first = jnp.stack([pay[0, pl.ds(4 + r, 8, stride=8)] for r in range(8)])
    lax.fori_loop(1, SLICES, link, first)

    for gather in gathers:
        gather.wait_send()
    for i in range(1, SLICES):
        @pl.when(n != i)
        def _():
            new_copy(i, column).wait_send()

    for k in range(SLICES):
        @pl.when((n != k) & (n > 0))
        def _():
            new_copy(k, flipped(k, side)).wait_recv()

    lane = lax.broadcasted_iota(jnp.int32, (CROWS, LANES), 1)
    for c in range(CT):
        new = jnp.where(
            lane < LANES // 2, pltpu.roll(newc[2 * c], LANES - 32, 1), pltpu.roll(newc[2 * c + 1], 32, 1)
        )
        was = coarse_old[c][...]
        change = jnp.where(n == 0, was, new) - was
        for i in range(4):
            spread_rows[pl.ds(BAND * c + i, CROWS, stride=4)] = change
    fine_change = matmul(spread_rows[...], grow[...])
    for c in range(CT):
        for m in range(4):
            for i in range(BAND // 8):
                out[i, 4 * c + m] = (
                    fine_end[4 * c + m, pl.ds(HALO + 8 * i, 8)]
                    + fine_change[BAND * c + 8 * i:BAND * c + 8 * (i + 1), m * LANES:(m + 1) * LANES]
                )


def per_device(states, stream):
    fine = pltpu.VMEM((FT, WIDE, LANES), F32)
    by_step = pltpu.VMEM((FINE_STEPS, FT, WIDE, LANES), F32)
    coarse = pltpu.VMEM((CT, 2 * CROWS, LANES), F32)

    def tiled(x):
        return x.reshape(BAND // 8, 8, FT, LANES).transpose(0, 2, 1, 3)

    ended = pl.pallas_call(
        kernel,
        out_shape=pltpu.VMEM((BAND // 8, FT, 8, LANES), F32),
        in_specs=[pl.BlockSpec(memory_space=pl.ANY)] * 2,
        out_specs=pl.BlockSpec(memory_space=pltpu.VMEM),
        scratch_shapes=[
            pltpu.VMEM((WIDE // 8, FT, 8, LANES), F32),
            pltpu.VMEM((WIDE // 8, FT, 8, LANES), F32),
            fine,
            pltpu.VMEM((FINE_STEPS + 1, FT, WIDE, LANES), F32),
            by_step, by_step, by_step,
            fine,
            fine,
            pltpu.VMEM((4 * LANES, LANES), jnp.bfloat16),
            pltpu.VMEM((LANES, 4 * LANES), jnp.bfloat16),
            pltpu.VMEM((2 * CT * 8, 4 * LANES), F32),
            coarse,
            coarse,
            coarse,
            pltpu.VMEM((5, CT, 2 * CROWS, LANES), F32),
            pltpu.VMEM((SLICES, CROWS, LANES), F32),
            pltpu.VMEM((SLICES, CROWS, LANES), F32),
            pltpu.VMEM((CWIDE, LANES), F32),
            pltpu.VMEM((SLICES - 1, CWIDE, LANES), F32),
            pltpu.VMEM((SLICES, CWIDE, LANES), F32),
            pltpu.VMEM((SLICES, CROWS, LANES), F32),
            pltpu.VMEM((CT * BAND, LANES), F32),
            pltpu.SemaphoreType.DMA((2,)),
            pltpu.SemaphoreType.DMA((4,)),
            pltpu.SemaphoreType.DMA((4,)),
            pltpu.SemaphoreType.DMA((2 * REACH,)),
            pltpu.SemaphoreType.DMA((2 * REACH,)),
            pltpu.SemaphoreType.DMA((SLICES,)),
            pltpu.SemaphoreType.DMA((SLICES,)),
            pltpu.SemaphoreType.DMA((2 * REACH,)),
            pltpu.SemaphoreType.DMA((2 * REACH,)),
            pltpu.SemaphoreType.DMA((SLICES,)),
            pltpu.SemaphoreType.DMA((SLICES,)),
        ],
        compiler_params=pltpu.CompilerParams(
            collective_id=0, has_side_effects=True, vmem_limit_bytes=60 * 1024 * 1024
        ),
    )(tiled(states), tiled(stream))
    return ended.transpose(0, 2, 1, 3).reshape(1, BAND, COLS)


def solution(mesh):
    in_specs = (P("cuts", "space", None), P("space", None))
    out_specs = P("cuts", "space", None)
    return jax.shard_map(
        per_device, mesh=mesh, in_specs=in_specs, out_specs=out_specs, check_vma=False
    )
```

```python
import jax
import jax.numpy as jnp
from jax import lax
from jax.experimental import pallas as pl
from jax.experimental.pallas import tpu as pltpu
from jax.sharding import PartitionSpec as P

MESH = pl.DeviceIdType.MESH
LANES = 128
COLS = 2048
FT = COLS // LANES
CT = FT // 4
BAND = 32
HALO = 16
WIDE = BAND + 2 * HALO
SLICES = 8
SPACE = 16
REACH = 4
CROWS = 8
CWIDE = CROWS * (2 * REACH + 1)
FINE_STEPS = 4
SPAN = 4
STAGES = 4 * FINE_STEPS
F32 = jnp.float32


def scales(step, kappa):
    gains = [step / (4 - s) / kappa for s in range(4)]
    betas = [1.0] * 4
    for s in (2, 1, 0):
        betas[s] = betas[s + 1] * gains[s + 1]
    return betas, betas[0] * gains[0]


FINE_BETAS, FINE_START = scales(0.25, 1.25)
COARSE_BETAS, COARSE_START = scales(1.0, 20.0)


def rows_up(t):
    return jnp.concatenate([t[1:], pltpu.roll(t[:1], 7, 1)], axis=0)


def rows_down(t):
    return jnp.concatenate([pltpu.roll(t[-1:], 1, 1), t[:-1]], axis=0)


def coefficients(psi, east, west):
    ce = 0.25 - 0.3125 * (rows_up(psi) - rows_down(psi))
    cn = 0.25 + 0.3125 * (east - west)
    return ce, cn


def operator(t, east, west, ce, cw, cn, cs):
    return ce * east + cw * west + cn * rows_up(t) + cs * rows_down(t) - t


def matmul(x, m):
    high = x.astype(jnp.bfloat16)
    x = x - high.astype(F32)
    middle = x.astype(jnp.bfloat16)
    low = (x - middle.astype(F32)).astype(jnp.bfloat16)
    small = jnp.dot(low, m, preferred_element_type=F32) + jnp.dot(middle, m, preferred_element_type=F32)
    return jnp.dot(high, m, preferred_element_type=F32) + small


def kernel(
    states, stream, out,
    xwin, swin, psi, field, field1, field2, field3, fce, fcn, shrink, grow, rows, cpsi, cce, ccn, cfield, wstream, wgap, spw, pay, nbuf, newc, spread_rows,
    local_sem, halo_send, halo_recv, sc_send, sc_recv, a_send, a_recv, b_send, b_recv, c_send, c_recv,
):
    n = lax.axis_index("cuts")
    b = lax.axis_index("space")

    def flipped(k, bit):
        return k + bit * (1 - 2 * lax.rem(k, 2))

    side = lax.rem(b // 2, 2)
    column = flipped(n, side)

    def at_space(j):
        return (n, lax.rem(b + (SPACE + j), SPACE))

    def at_window(j):
        other = lax.rem(b + (SPACE + j), SPACE)
        return (flipped(n, lax.rem(side + lax.rem(other // 2, 2), 2)), other)

    across = 2 * lax.rem(b, 2) - 1
    offsets = [(1, across)] + [(d, j) for d in range(2, REACH + 1) for j in (-d, d)] + [(1, -across)]
    others = [lax.rem(n + k, SLICES) for k in (4, 5, 3, 2, 6, 1, 7)]


    own_x = pltpu.make_async_copy(states, xwin.at[pl.ds(HALO // 8, BAND // 8)], local_sem.at[0])
    own_s = pltpu.make_async_copy(stream, swin.at[pl.ds(HALO // 8, BAND // 8)], local_sem.at[1])
    own_s.start()
    own_x.start()

    pay[...] = jnp.zeros_like(pay)
    newc[...] = jnp.zeros_like(newc)

    barrier = pltpu.get_barrier_semaphore()
    greeted = [at_space(across)]
    greeted += [(k, b) for k in others]
    greeted += [at_window(j) for _, j in offsets]
    for device in greeted:
        pl.semaphore_signal(barrier, inc=1, device_id=device, device_id_type=MESH)
    pl.semaphore_wait(barrier, len(greeted))

    halos = []
    for at, (source, window, device) in enumerate(((stream, swin, at_space), (states, xwin, at_space))):
        for end, (j, first, target) in enumerate(((1, BAND - HALO, 0), (-1, 0, HALO + BAND))):
            halos.append(
                pltpu.make_async_remote_copy(
                    src_ref=source.at[pl.ds(first // 8, HALO // 8)],
                    dst_ref=window.at[pl.ds(target // 8, HALO // 8)],
                    send_sem=halo_send.at[2 * at + end],
                    recv_sem=halo_recv.at[2 * at + end],
                    device_id=device(j),
                    device_id_type=MESH,
                )
            )
            halos[-1].start()

    fine_at = lax.broadcasted_iota(jnp.int32, (4 * LANES, LANES), 0)
    coarse_at = lax.broadcasted_iota(jnp.int32, (4 * LANES, LANES), 1)
    shrink[...] = jnp.where((fine_at >> 2) == coarse_at, 0.0625, 0.0).astype(jnp.bfloat16)
    fine_at = lax.broadcasted_iota(jnp.int32, (LANES, 4 * LANES), 1)
    coarse_at = lax.broadcasted_iota(jnp.int32, (LANES, 4 * LANES), 0)
    grow[...] = jnp.where((fine_at >> 2) == coarse_at, 1.0, 0.0).astype(jnp.bfloat16)

    def windows(tiles, target):
        lane = lax.broadcasted_iota(jnp.int32, (CROWS, LANES), 1)
        right = [pltpu.roll(t, 32, 1) for t in tiles]
        left = [pltpu.roll(t, LANES - 32, 1) for t in tiles]
        for j in range(CT):
            target[2 * j] = jnp.where(lane < 32, right[(j - 1) % CT], right[j])
            target[2 * j + 1] = jnp.where(lane < LANES - 32, left[j], left[(j + 1) % CT])

    own = range(HALO // 8, (HALO + BAND) // 8)
    around = [i for i in range(WIDE // 8) if i not in own]

    def untile(window, target, parts):
        for i in parts:
            for c in range(FT):
                target[c, pl.ds(8 * i, 8)] = window[i, c]

    def add_rows(source, at, first):
        for c in range(FT):
            parts = [source[c, pl.ds(first + i, 8, stride=4)] for i in range(4)]
            rows[pl.ds(at(c // 4), 8), pl.ds(c % 4 * LANES, LANES)] = parts[0] + parts[1] + (parts[2] + parts[3])

    def restricted_band(source):
        add_rows(source, lambda c: CROWS * c, HALO)
        small = matmul(rows[pl.ds(0, CROWS * CT)], shrink[...])
        return [small[CROWS * c:CROWS * (c + 1)] for c in range(CT)]

    def restricted_window(source, target):
        for half in range(2):
            add_rows(source, lambda c: 2 * CROWS * c + CROWS * half, half * WIDE // 2)
        small = matmul(rows[...], shrink[...])
        for c in range(CT):
            target[c] = small[2 * CROWS * c:2 * CROWS * (c + 1)]

    own_s.wait()
    untile(swin, psi, own)
    windows(restricted_band(psi), wstream)
    spreads = []
    for at, (_, j) in enumerate(offsets):
        spreads.append(
            pltpu.make_async_remote_copy(
                src_ref=wstream.at[column],
                dst_ref=spw.at[pl.ds(pl.multiple_of(CROWS * (REACH - j), CROWS), CROWS)],
                send_sem=sc_send.at[at],
                recv_sem=sc_recv.at[at],
                device_id=at_window(j),
                device_id_type=MESH,
            )
        )
        spreads[-1].start()
    spw[pl.ds(CROWS * REACH, CROWS)] = wstream[column]
    own_x.wait()

    def first_lane(t):
        return lax.broadcasted_iota(jnp.int32, t.shape, 1) == 0

    def last_lane(t):
        return lax.broadcasted_iota(jnp.int32, t.shape, 1) == LANES - 1

    def wrapped(c):
        return c % FT if isinstance(c, int) else lax.rem(c, FT)

    def over_tiles(source, blocks, tiles, work):
        def west_of(c):
            return [pltpu.roll(source[c, pl.ds(*block)], 1, 1) for block in blocks]

        def east_of(c):
            return [pltpu.roll(source[c, pl.ds(*block)], LANES - 1, 1) for block in blocks]

        before, now = west_of(wrapped(tiles[0] + FT - 1)), east_of(tiles[0])
        for c in tiles:
            west_now, after = west_of(c), east_of(wrapped(c + 1))
            for i, block in enumerate(blocks):
                t = source[c, pl.ds(*block)]
                west = jnp.where(first_lane(t), before[i], west_now[i])
                east = jnp.where(last_lane(t), after[i], now[i])
                work(c, block, t, east, west)
            before, now = west_now, after

    def shifted(source, c, block, by):
        return source[c, pl.ds(block[0] + by, block[1])]

    def weigh(c, block, t, east, west):
        fce[c, pl.ds(*block)] = 0.25 - 0.3125 * (shifted(psi, c, block, 1) - shifted(psi, c, block, -1))
        fcn[c, pl.ds(*block)] = 0.25 + 0.3125 * (east - west)

    stages = [field, field1, field2, field3]

    def stage(step, s, blocks, tiles):
        source, base = stages[s].at[step], field.at[step]
        target = stages[s + 1].at[step] if s < 3 else field.at[step + 1]

        def work(c, block, t, east, west):
            here = pl.ds(*block)
            up, down = shifted(source, c, block, 1), shifted(source, c, block, -1)
            change = (fcn[c, here] * (up - down) + (0.5 * down - t)) + (fce[c, here] * (east - west) + 0.5 * west)
            if s == 0:
                change = FINE_START * change
            target[c, here] = FINE_BETAS[s] * base[c, here] + change

        over_tiles(source, blocks, tiles, work)

    def blocks_of(first, last):
        count = max((last - first + 7) // 8, 1)
        return [(first + 8 * i, 8) for i in range(count - 1)] + [(max(last - 8, first), 8)]

    def by_runs(work):
        def run(at, carry):
            work([at * SPAN + i for i in range(SPAN)])
            return carry

        lax.fori_loop(0, FT // SPAN, run, 0)

    untile(xwin, field.at[0], own)
    by_runs(lambda tiles: over_tiles(psi, blocks_of(HALO + 1, HALO + BAND - 1), tiles, weigh))
    for k in range(STAGES - 1):
        inner = blocks_of(HALO + k + 1, HALO + BAND - k - 1)
        by_runs(lambda tiles: stage(k // 4, k % 4, inner, tiles))

    for halo in halos[:2]:
        halo.wait_recv()
    untile(swin, psi, around)
    over_tiles(psi, [(1, HALO), (WIDE - 1 - HALO, HALO)], range(FT), weigh)
    restricted_window(psi, cpsi)
    middle_rows = [(1, 8), (7, 8)]
    for c in range(CT):
        for block in middle_rows:
            t = [cpsi[(c + d) % CT, pl.ds(*block)] for d in (-1, 0, 1)]
            west = jnp.where(first_lane(t[1]), pltpu.roll(t[0], 1, 1), pltpu.roll(t[1], 1, 1))
            east = jnp.where(last_lane(t[1]), pltpu.roll(t[2], LANES - 1, 1), pltpu.roll(t[1], LANES - 1, 1))
            cce[c, pl.ds(*block)] = 0.25 - 0.3125 * (shifted(cpsi, c, block, 1) - shifted(cpsi, c, block, -1))
            ccn[c, pl.ds(*block)] = 0.25 + 0.3125 * (east - west)

    for halo in halos[2:]:
        halo.wait_recv()
    untile(xwin, field.at[0], around)

    restricted_window(field.at[0], cfield.at[0])
    for s in range(4):
        for c in range(CT):
            for block in [(s + 1, 8), (7 - s, 8)][:2 if s < 3 else 1]:
                here = pl.ds(*block)
                t = [cfield[s, (c + d) % CT, here] for d in (-1, 0, 1)]
                west = jnp.where(first_lane(t[1]), pltpu.roll(t[0], 1, 1), pltpu.roll(t[1], 1, 1))
                east = jnp.where(last_lane(t[1]), pltpu.roll(t[2], LANES - 1, 1), pltpu.roll(t[1], LANES - 1, 1))
                up, down = shifted(cfield.at[s], c, block, 1), shifted(cfield.at[s], c, block, -1)
                change = ccn[c, here] * (up - down) + (0.5 * (west + down) - t[1]) + cce[c, here] * (east - west)
                if s == 0:
                    change = COARSE_START * change
                cfield[s + 1, c, here] = COARSE_BETAS[s] * cfield[0, c, here] + change
    coarse_old = [cfield.at[4, c, pl.ds(4, CROWS)] for c in range(CT)]

    for step in range(FINE_STEPS):
        for s in range(4):
            done = 4 * step + s
            blocks = [(done + 1, HALO), (WIDE - HALO - 1 - done, HALO)]
            stage(step, s, blocks, [(c + s) % FT for c in range(FT)])
    fine_end = field.at[FINE_STEPS]

    ended = restricted_band(fine_end)
    gap = [ended[c] - coarse_old[c][...] for c in range(CT)]
    windows([jnp.where(n == 0, coarse_old[c][...] + gap[c], gap[c]) for c in range(CT)], wgap)

    middle = pl.ds(CROWS * REACH, CROWS)

    def gap_copy(k, m):
        return pltpu.make_async_remote_copy(
            src_ref=wgap.at[flipped(k, side)],
            dst_ref=pay.at[m, middle],
            send_sem=a_send.at[k],
            recv_sem=a_recv.at[m],
            device_id=(k, b),
            device_id_type=MESH,
        )

    @pl.when(n < SLICES - 1)
    def _():
        for k in others:
            gap_copy(k, n).start()
        pay[n, middle] = wgap[column]

    for spread in spreads:
        spread.wait()
    around_psi = jnp.stack([spw[pl.ds(4 + r, 8, stride=8)] for r in range(8)])
    ce, cn = coefficients(
        around_psi, pltpu.roll(around_psi, LANES - 1, 2), pltpu.roll(around_psi, 1, 2)
    )
    chain_weights = (ce, 0.5 - ce, cn, 0.5 - cn)

    for m in range(SLICES - 1):
        @pl.when(n != m)
        def _():
            gap_copy(m, m).wait_recv()

    gathers = []
    for at, (distance, j) in enumerate(offsets):
        count = SLICES + 1 - 2 * distance
        gathers.append(
            pltpu.make_async_remote_copy(
                src_ref=pay.at[pl.ds(0, count), middle],
                dst_ref=pay.at[pl.ds(0, count), pl.ds(pl.multiple_of(CROWS * (REACH - j), CROWS), CROWS)],
                send_sem=b_send.at[at],
                recv_sem=b_recv.at[at],
                device_id=at_window(j),
                device_id_type=MESH,
            )
        )
        gathers[-1].start()

    for halo in halos:
        halo.wait_send()

    @pl.when(n < SLICES - 1)
    def _():
        for k in others:
            gap_copy(k, n).wait_send()

    for gather in gathers:
        gather.wait_recv()

    def new_copy(i, window):
        return pltpu.make_async_remote_copy(
            src_ref=nbuf.at[i, middle],
            dst_ref=newc.at[window],
            send_sem=c_send.at[i],
            recv_sem=c_recv.at[window],
            device_id=(i, b),
            device_id_type=MESH,
        )

    def link(i, current):
        t = current
        for s in range(4):
            change = operator(t, pltpu.roll(t, LANES - 1, 2), pltpu.roll(t, 1, 2), *chain_weights)
            if s == 0:
                change = COARSE_START * change
            t = COARSE_BETAS[s] * current + change
        for r in range(8):
            nbuf[i, pl.ds(4 + r, 8, stride=8)] = t[r]

        @pl.when(i != n)
        def _():
            new_copy(i, column).start()

        @pl.when(i == n)
        def _():
            newc[column] = nbuf[i, middle]

        late = lax.rem(i, SLICES - 1)
        return t + jnp.stack([pay[late, pl.ds(4 + r, 8, stride=8)] for r in range(8)])

    first = jnp.stack([pay[0, pl.ds(4 + r, 8, stride=8)] for r in range(8)])
    lax.fori_loop(1, SLICES, link, first)

    for gather in gathers:
        gather.wait_send()
    for i in range(1, SLICES):
        @pl.when(n != i)
        def _():
            new_copy(i, column).wait_send()

    for k in range(SLICES):
        @pl.when((n != k) & (n > 0))
        def _():
            new_copy(k, flipped(k, side)).wait_recv()

    lane = lax.broadcasted_iota(jnp.int32, (CROWS, LANES), 1)
    for c in range(CT):
        new = jnp.where(
            lane < LANES // 2, pltpu.roll(newc[2 * c], LANES - 32, 1), pltpu.roll(newc[2 * c + 1], 32, 1)
        )
        was = coarse_old[c][...]
        change = jnp.where(n == 0, was, new) - was
        for i in range(4):
            spread_rows[pl.ds(BAND * c + i, CROWS, stride=4)] = change
    fine_change = matmul(spread_rows[...], grow[...])
    for c in range(CT):
        for m in range(4):
            for i in range(BAND // 8):
                out[i, 4 * c + m] = (
                    fine_end[4 * c + m, pl.ds(HALO + 8 * i, 8)]
                    + fine_change[BAND * c + 8 * i:BAND * c + 8 * (i + 1), m * LANES:(m + 1) * LANES]
                )


def per_device(states, stream):
    fine = pltpu.VMEM((FT, WIDE, LANES), F32)
    by_step = pltpu.VMEM((FINE_STEPS, FT, WIDE, LANES), F32)
    coarse = pltpu.VMEM((CT, 2 * CROWS, LANES), F32)

    def tiled(x):
        return x.reshape(BAND // 8, 8, FT, LANES).transpose(0, 2, 1, 3)

    ended = pl.pallas_call(
        kernel,
        out_shape=pltpu.VMEM((BAND // 8, FT, 8, LANES), F32),
        in_specs=[pl.BlockSpec(memory_space=pl.ANY)] * 2,
        out_specs=pl.BlockSpec(memory_space=pltpu.VMEM),
        scratch_shapes=[
            pltpu.VMEM((WIDE // 8, FT, 8, LANES), F32),
            pltpu.VMEM((WIDE // 8, FT, 8, LANES), F32),
            fine,
            pltpu.VMEM((FINE_STEPS + 1, FT, WIDE, LANES), F32),
            by_step, by_step, by_step,
            fine,
            fine,
            pltpu.VMEM((4 * LANES, LANES), jnp.bfloat16),
            pltpu.VMEM((LANES, 4 * LANES), jnp.bfloat16),
            pltpu.VMEM((2 * CT * 8, 4 * LANES), F32),
            coarse,
            coarse,
            coarse,
            pltpu.VMEM((5, CT, 2 * CROWS, LANES), F32),
            pltpu.VMEM((SLICES, CROWS, LANES), F32),
            pltpu.VMEM((SLICES, CROWS, LANES), F32),
            pltpu.VMEM((CWIDE, LANES), F32),
            pltpu.VMEM((SLICES - 1, CWIDE, LANES), F32),
            pltpu.VMEM((SLICES, CWIDE, LANES), F32),
            pltpu.VMEM((SLICES, CROWS, LANES), F32),
            pltpu.VMEM((CT * BAND, LANES), F32),
            pltpu.SemaphoreType.DMA((2,)),
            pltpu.SemaphoreType.DMA((4,)),
            pltpu.SemaphoreType.DMA((4,)),
            pltpu.SemaphoreType.DMA((2 * REACH,)),
            pltpu.SemaphoreType.DMA((2 * REACH,)),
            pltpu.SemaphoreType.DMA((SLICES,)),
            pltpu.SemaphoreType.DMA((SLICES,)),
            pltpu.SemaphoreType.DMA((2 * REACH,)),
            pltpu.SemaphoreType.DMA((2 * REACH,)),
            pltpu.SemaphoreType.DMA((SLICES,)),
            pltpu.SemaphoreType.DMA((SLICES,)),
        ],
        compiler_params=pltpu.CompilerParams(
            collective_id=0, has_side_effects=True, vmem_limit_bytes=60 * 1024 * 1024
        ),
    )(tiled(states), tiled(stream))
    return ended.transpose(0, 2, 1, 3).reshape(1, BAND, COLS)


def solution(mesh):
    in_specs = (P("cuts", "space", None), P("space", None))
    out_specs = P("cuts", "space", None)
    return jax.shard_map(
        per_device, mesh=mesh, in_specs=in_specs, out_specs=out_specs, check_vma=False
    )
```

```python
import jax
import jax.numpy as jnp
from jax import lax
from jax.experimental import pallas as pl
from jax.experimental.pallas import tpu as pltpu
from jax.sharding import PartitionSpec as P

MESH = pl.DeviceIdType.MESH
LANES = 128
COLS = 2048
FT = COLS // LANES
CT = FT // 4
BAND = 32
HALO = 16
WIDE = BAND + 2 * HALO
SLICES = 8
SPACE = 16
REACH = 4
CROWS = 8
CWIDE = CROWS * (2 * REACH + 1)
FINE_STEPS = 4
SPAN = 4
STAGES = 4 * FINE_STEPS
F32 = jnp.float32


def scales(step, kappa):
    gains = [step / (4 - s) / kappa for s in range(4)]
    betas = [1.0] * 4
    for s in (2, 1, 0):
        betas[s] = betas[s + 1] * gains[s + 1]
    return betas, betas[0] * gains[0]


FINE_BETAS, FINE_START = scales(0.25, 1.25)
COARSE_BETAS, COARSE_START = scales(1.0, 20.0)


def rows_up(t):
    return jnp.concatenate([t[1:], pltpu.roll(t[:1], 7, 1)], axis=0)


def rows_down(t):
    return jnp.concatenate([pltpu.roll(t[-1:], 1, 1), t[:-1]], axis=0)


def coefficients(psi, east, west):
    ce = 0.25 - 0.3125 * (rows_up(psi) - rows_down(psi))
    cn = 0.25 + 0.3125 * (east - west)
    return ce, cn


def operator(t, east, west, ce, cw, cn, cs):
    return ce * east + cw * west + cn * rows_up(t) + cs * rows_down(t) - t


def matmul(x, m):
    high = x.astype(jnp.bfloat16)
    x = x - high.astype(F32)
    middle = x.astype(jnp.bfloat16)
    low = (x - middle.astype(F32)).astype(jnp.bfloat16)
    small = jnp.dot(low, m, preferred_element_type=F32) + jnp.dot(middle, m, preferred_element_type=F32)
    return jnp.dot(high, m, preferred_element_type=F32) + small


def kernel(
    states, stream, out,
    xwin, swin, psi, field, field1, field2, field3, fce, fcn, shrink, grow, rows, cpsi, cce, ccn, cfield, wstream, wgap, spw, pay, nbuf, newc, spread_rows,
    local_sem, halo_send, halo_recv, sc_send, sc_recv, a_send, a_recv, b_send, b_recv, c_send, c_recv,
):
    n = lax.axis_index("cuts")
    b = lax.axis_index("space")

    def flipped(k, bit):
        return k + bit * (1 - 2 * lax.rem(k, 2))

    side = lax.rem(b // 2, 2)
    column = flipped(n, side)

    def at_space(j):
        return (n, lax.rem(b + (SPACE + j), SPACE))

    def at_window(j):
        other = lax.rem(b + (SPACE + j), SPACE)
        return (flipped(n, lax.rem(side + lax.rem(other // 2, 2), 2)), other)

    across = 2 * lax.rem(b, 2) - 1
    offsets = [(1, across)] + [(d, j) for d in range(2, REACH + 1) for j in (-d, d)] + [(1, -across)]
    others = [lax.rem(n + k, SLICES) for k in (4, 5, 3, 2, 6, 1, 7)]


    own_x = pltpu.make_async_copy(states, xwin.at[pl.ds(HALO // 8, BAND // 8)], local_sem.at[0])
    own_s = pltpu.make_async_copy(stream, swin.at[pl.ds(HALO // 8, BAND // 8)], local_sem.at[1])
    own_s.start()
    own_x.start()

    pay[...] = jnp.zeros_like(pay)
    newc[...] = jnp.zeros_like(newc)

    barrier = pltpu.get_barrier_semaphore()
    greeted = [at_space(across)]
    greeted += [(k, b) for k in others]
    greeted += [at_window(j) for _, j in offsets]
    for device in greeted:
        pl.semaphore_signal(barrier, inc=1, device_id=device, device_id_type=MESH)
    pl.semaphore_wait(barrier, len(greeted))

    halos = []
    for at, (source, window, device) in enumerate(((stream, swin, at_space), (states, xwin, at_space))):
        for end, (j, first, target) in enumerate(((1, BAND - HALO, 0), (-1, 0, HALO + BAND))):
            halos.append(
                pltpu.make_async_remote_copy(
                    src_ref=source.at[pl.ds(first // 8, HALO // 8)],
                    dst_ref=window.at[pl.ds(target // 8, HALO // 8)],
                    send_sem=halo_send.at[2 * at + end],
                    recv_sem=halo_recv.at[2 * at + end],
                    device_id=device(j),
                    device_id_type=MESH,
                )
            )
            halos[-1].start()

    fine_at = lax.broadcasted_iota(jnp.int32, (4 * LANES, LANES), 0)
    coarse_at = lax.broadcasted_iota(jnp.int32, (4 * LANES, LANES), 1)
    shrink[...] = jnp.where((fine_at >> 2) == coarse_at, 0.0625, 0.0).astype(jnp.bfloat16)
    fine_at = lax.broadcasted_iota(jnp.int32, (LANES, 4 * LANES), 1)
    coarse_at = lax.broadcasted_iota(jnp.int32, (LANES, 4 * LANES), 0)
    grow[...] = jnp.where((fine_at >> 2) == coarse_at, 1.0, 0.0).astype(jnp.bfloat16)

    def windows(tiles, target):
        lane = lax.broadcasted_iota(jnp.int32, (CROWS, LANES), 1)
        right = [pltpu.roll(t, 32, 1) for t in tiles]
        left = [pltpu.roll(t, LANES - 32, 1) for t in tiles]
        for j in range(CT):
            target[2 * j] = jnp.where(lane < 32, right[(j - 1) % CT], right[j])
            target[2 * j + 1] = jnp.where(lane < LANES - 32, left[j], left[(j + 1) % CT])

    own = range(HALO // 8, (HALO + BAND) // 8)
    around = [i for i in range(WIDE // 8) if i not in own]

    def untile(window, target, parts):
        for i in parts:
            for c in range(FT):
                target[c, pl.ds(8 * i, 8)] = window[i, c]

    def add_rows(source, at, first):
        for c in range(FT):
            parts = [source[c, pl.ds(first + i, 8, stride=4)] for i in range(4)]
            rows[pl.ds(at(c // 4), 8), pl.ds(c % 4 * LANES, LANES)] = parts[0] + parts[1] + (parts[2] + parts[3])

    def restricted_band(source):
        add_rows(source, lambda c: CROWS * c, HALO)
        small = matmul(rows[pl.ds(0, CROWS * CT)], shrink[...])
        return [small[CROWS * c:CROWS * (c + 1)] for c in range(CT)]

    def restricted_window(source, target):
        for half in range(2):
            add_rows(source, lambda c: 2 * CROWS * c + CROWS * half, half * WIDE // 2)
        small = matmul(rows[...], shrink[...])
        for c in range(CT):
            target[c] = small[2 * CROWS * c:2 * CROWS * (c + 1)]

    own_s.wait()
    untile(swin, psi, own)
    windows(restricted_band(psi), wstream)
    spreads = []
    for at, (_, j) in enumerate(offsets):
        spreads.append(
            pltpu.make_async_remote_copy(
                src_ref=wstream.at[column],
                dst_ref=spw.at[pl.ds(pl.multiple_of(CROWS * (REACH - j), CROWS), CROWS)],
                send_sem=sc_send.at[at],
                recv_sem=sc_recv.at[at],
                device_id=at_window(j),
                device_id_type=MESH,
            )
        )
        spreads[-1].start()
    spw[pl.ds(CROWS * REACH, CROWS)] = wstream[column]
    own_x.wait()

    def first_lane(t):
        return lax.broadcasted_iota(jnp.int32, t.shape, 1) == 0

    def last_lane(t):
        return lax.broadcasted_iota(jnp.int32, t.shape, 1) == LANES - 1

    def wrapped(c):
        return c % FT if isinstance(c, int) else lax.rem(c, FT)

    def over_tiles(source, blocks, tiles, work):
        def west_of(c):
            return [pltpu.roll(source[c, pl.ds(*block)], 1, 1) for block in blocks]

        def east_of(c):
            return [pltpu.roll(source[c, pl.ds(*block)], LANES - 1, 1) for block in blocks]

        before, now = west_of(wrapped(tiles[0] + FT - 1)), east_of(tiles[0])
        for c in tiles:
            west_now, after = west_of(c), east_of(wrapped(c + 1))
            for i, block in enumerate(blocks):
                t = source[c, pl.ds(*block)]
                west = jnp.where(first_lane(t), before[i], west_now[i])
                east = jnp.where(last_lane(t), after[i], now[i])
                work(c, block, t, east, west)
            before, now = west_now, after

    def shifted(source, c, block, by):
        return source[c, pl.ds(block[0] + by, block[1])]

    def weigh(c, block, t, east, west):
        fce[c, pl.ds(*block)] = 0.25 - 0.3125 * (shifted(psi, c, block, 1) - shifted(psi, c, block, -1))
        fcn[c, pl.ds(*block)] = 0.25 + 0.3125 * (east - west)

    stages = [field, field1, field2, field3]

    def stage(step, s, blocks, tiles):
        source, base = stages[s].at[step], field.at[step]
        target = stages[s + 1].at[step] if s < 3 else field.at[step + 1]

        def work(c, block, t, east, west):
            here = pl.ds(*block)
            up, down = shifted(source, c, block, 1), shifted(source, c, block, -1)
            change = (fcn[c, here] * (up - down) + (0.5 * down - t)) + (fce[c, here] * (east - west) + 0.5 * west)
            if s == 0:
                change = FINE_START * change
            target[c, here] = FINE_BETAS[s] * base[c, here] + change

        over_tiles(source, blocks, tiles, work)

    def blocks_of(first, last):
        count = max((last - first + 7) // 8, 1)
        return [(first + 8 * i, 8) for i in range(count - 1)] + [(max(last - 8, first), 8)]

    def by_runs(work):
        def run(at, carry):
            work([at * SPAN + i for i in range(SPAN)])
            return carry

        lax.fori_loop(0, FT // SPAN, run, 0)

    untile(xwin, field.at[0], own)
    by_runs(lambda tiles: over_tiles(psi, blocks_of(HALO + 1, HALO + BAND - 1), tiles, weigh))
    for k in range(STAGES - 1):
        inner = blocks_of(HALO + k + 1, HALO + BAND - k - 1)
        by_runs(lambda tiles: stage(k // 4, k % 4, inner, tiles))

    for halo in halos[:2]:
        halo.wait_recv()
    untile(swin, psi, around)
    over_tiles(psi, [(1, HALO), (WIDE - 1 - HALO, HALO)], range(FT), weigh)
    restricted_window(psi, cpsi)
    middle_rows = [(1, 8), (7, 8)]
    for c in range(CT):
        for block in middle_rows:
            t = [cpsi[(c + d) % CT, pl.ds(*block)] for d in (-1, 0, 1)]
            west = jnp.where(first_lane(t[1]), pltpu.roll(t[0], 1, 1), pltpu.roll(t[1], 1, 1))
            east = jnp.where(last_lane(t[1]), pltpu.roll(t[2], LANES - 1, 1), pltpu.roll(t[1], LANES - 1, 1))
            cce[c, pl.ds(*block)] = 0.25 - 0.3125 * (shifted(cpsi, c, block, 1) - shifted(cpsi, c, block, -1))
            ccn[c, pl.ds(*block)] = 0.25 + 0.3125 * (east - west)

    for halo in halos[2:]:
        halo.wait_recv()
    untile(xwin, field.at[0], around)

    restricted_window(field.at[0], cfield.at[0])
    for s in range(4):
        for c in range(CT):
            for block in [(s + 1, 8), (7 - s, 8)][:2 if s < 3 else 1]:
                here = pl.ds(*block)
                t = [cfield[s, (c + d) % CT, here] for d in (-1, 0, 1)]
                west = jnp.where(first_lane(t[1]), pltpu.roll(t[0], 1, 1), pltpu.roll(t[1], 1, 1))
                east = jnp.where(last_lane(t[1]), pltpu.roll(t[2], LANES - 1, 1), pltpu.roll(t[1], LANES - 1, 1))
                up, down = shifted(cfield.at[s], c, block, 1), shifted(cfield.at[s], c, block, -1)
                change = (ccn[c, here] * (up - down) + (0.5 * down - t[1])) + (cce[c, here] * (east - west) + 0.5 * west)
                if s == 0:
                    change = COARSE_START * change
                cfield[s + 1, c, here] = COARSE_BETAS[s] * cfield[0, c, here] + change
    coarse_old = [cfield.at[4, c, pl.ds(4, CROWS)] for c in range(CT)]

    for step in range(FINE_STEPS):
        for s in range(4):
            done = 4 * step + s
            blocks = [(done + 1, HALO), (WIDE - HALO - 1 - done, HALO)]
            stage(step, s, blocks, [(c + s) % FT for c in range(FT)])
    fine_end = field.at[FINE_STEPS]

    ended = restricted_band(fine_end)
    gap = [ended[c] - coarse_old[c][...] for c in range(CT)]
    windows([jnp.where(n == 0, coarse_old[c][...] + gap[c], gap[c]) for c in range(CT)], wgap)

    middle = pl.ds(CROWS * REACH, CROWS)

    def gap_copy(k, m):
        return pltpu.make_async_remote_copy(
            src_ref=wgap.at[flipped(k, side)],
            dst_ref=pay.at[m, middle],
            send_sem=a_send.at[k],
            recv_sem=a_recv.at[m],
            device_id=(k, b),
            device_id_type=MESH,
        )

    @pl.when(n < SLICES - 1)
    def _():
        for k in others:
            gap_copy(k, n).start()
        pay[n, middle] = wgap[column]

    for spread in spreads:
        spread.wait()
    around_psi = jnp.stack([spw[pl.ds(4 + r, 8, stride=8)] for r in range(8)])
    ce, cn = coefficients(
        around_psi, pltpu.roll(around_psi, LANES - 1, 2), pltpu.roll(around_psi, 1, 2)
    )
    chain_weights = (ce, 0.5 - ce, cn, 0.5 - cn)

    for m in range(SLICES - 1):
        @pl.when(n != m)
        def _():
            gap_copy(m, m).wait_recv()

    gathers = []
    for at, (distance, j) in enumerate(offsets):
        count = SLICES + 1 - 2 * distance
        gathers.append(
            pltpu.make_async_remote_copy(
                src_ref=pay.at[pl.ds(0, count), middle],
                dst_ref=pay.at[pl.ds(0, count), pl.ds(pl.multiple_of(CROWS * (REACH - j), CROWS), CROWS)],
                send_sem=b_send.at[at],
                recv_sem=b_recv.at[at],
                device_id=at_window(j),
                device_id_type=MESH,
            )
        )
        gathers[-1].start()

    for halo in halos:
        halo.wait_send()

    @pl.when(n < SLICES - 1)
    def _():
        for k in others:
            gap_copy(k, n).wait_send()

    for gather in gathers:
        gather.wait_recv()

    def new_copy(i, window):
        return pltpu.make_async_remote_copy(
            src_ref=nbuf.at[i, middle],
            dst_ref=newc.at[window],
            send_sem=c_send.at[i],
            recv_sem=c_recv.at[window],
            device_id=(i, b),
            device_id_type=MESH,
        )

    def link(i, current):
        t = current
        for s in range(4):
            ce, cw, cn, cs = chain_weights
            east, west = pltpu.roll(t, LANES - 1, 2), pltpu.roll(t, 1, 2)
            rest, turned = cn * rows_up(t) + cs * rows_down(t) - t, ce * east + cw * west
            if s == 0:
                t = COARSE_BETAS[s] * current + COARSE_START * (rest + turned)
            else:
                t = (COARSE_BETAS[s] * current + rest) + turned
        for r in range(8):
            nbuf[i, pl.ds(4 + r, 8, stride=8)] = t[r]

        @pl.when(i != n)
        def _():
            new_copy(i, column).start()

        @pl.when(i == n)
        def _():
            newc[column] = nbuf[i, middle]

        late = lax.rem(i, SLICES - 1)
        return t + jnp.stack([pay[late, pl.ds(4 + r, 8, stride=8)] for r in range(8)])

    first = jnp.stack([pay[0, pl.ds(4 + r, 8, stride=8)] for r in range(8)])
    lax.fori_loop(1, SLICES, link, first)

    for gather in gathers:
        gather.wait_send()
    for i in range(1, SLICES):
        @pl.when(n != i)
        def _():
            new_copy(i, column).wait_send()

    for k in range(SLICES):
        @pl.when((n != k) & (n > 0))
        def _():
            new_copy(k, flipped(k, side)).wait_recv()

    lane = lax.broadcasted_iota(jnp.int32, (CROWS, LANES), 1)
    for c in range(CT):
        new = jnp.where(
            lane < LANES // 2, pltpu.roll(newc[2 * c], LANES - 32, 1), pltpu.roll(newc[2 * c + 1], 32, 1)
        )
        was = coarse_old[c][...]
        change = jnp.where(n == 0, was, new) - was
        for i in range(4):
            spread_rows[pl.ds(BAND * c + i, CROWS, stride=4)] = change
    fine_change = matmul(spread_rows[...], grow[...])
    for c in range(CT):
        for m in range(4):
            for i in range(BAND // 8):
                out[i, 4 * c + m] = (
                    fine_end[4 * c + m, pl.ds(HALO + 8 * i, 8)]
                    + fine_change[BAND * c + 8 * i:BAND * c + 8 * (i + 1), m * LANES:(m + 1) * LANES]
                )


def per_device(states, stream):
    fine = pltpu.VMEM((FT, WIDE, LANES), F32)
    by_step = pltpu.VMEM((FINE_STEPS, FT, WIDE, LANES), F32)
    coarse = pltpu.VMEM((CT, 2 * CROWS, LANES), F32)

    def tiled(x):
        return x.reshape(BAND // 8, 8, FT, LANES).transpose(0, 2, 1, 3)

    ended = pl.pallas_call(
        kernel,
        out_shape=pltpu.VMEM((BAND // 8, FT, 8, LANES), F32),
        in_specs=[pl.BlockSpec(memory_space=pl.ANY)] * 2,
        out_specs=pl.BlockSpec(memory_space=pltpu.VMEM),
        scratch_shapes=[
            pltpu.VMEM((WIDE // 8, FT, 8, LANES), F32),
            pltpu.VMEM((WIDE // 8, FT, 8, LANES), F32),
            fine,
            pltpu.VMEM((FINE_STEPS + 1, FT, WIDE, LANES), F32),
            by_step, by_step, by_step,
            fine,
            fine,
            pltpu.VMEM((4 * LANES, LANES), jnp.bfloat16),
            pltpu.VMEM((LANES, 4 * LANES), jnp.bfloat16),
            pltpu.VMEM((2 * CT * 8, 4 * LANES), F32),
            coarse,
            coarse,
            coarse,
            pltpu.VMEM((5, CT, 2 * CROWS, LANES), F32),
            pltpu.VMEM((SLICES, CROWS, LANES), F32),
            pltpu.VMEM((SLICES, CROWS, LANES), F32),
            pltpu.VMEM((CWIDE, LANES), F32),
            pltpu.VMEM((SLICES - 1, CWIDE, LANES), F32),
            pltpu.VMEM((SLICES, CWIDE, LANES), F32),
            pltpu.VMEM((SLICES, CROWS, LANES), F32),
            pltpu.VMEM((CT * BAND, LANES), F32),
            pltpu.SemaphoreType.DMA((2,)),
            pltpu.SemaphoreType.DMA((4,)),
            pltpu.SemaphoreType.DMA((4,)),
            pltpu.SemaphoreType.DMA((2 * REACH,)),
            pltpu.SemaphoreType.DMA((2 * REACH,)),
            pltpu.SemaphoreType.DMA((SLICES,)),
            pltpu.SemaphoreType.DMA((SLICES,)),
            pltpu.SemaphoreType.DMA((2 * REACH,)),
            pltpu.SemaphoreType.DMA((2 * REACH,)),
            pltpu.SemaphoreType.DMA((SLICES,)),
            pltpu.SemaphoreType.DMA((SLICES,)),
        ],
        compiler_params=pltpu.CompilerParams(
            collective_id=0, has_side_effects=True, vmem_limit_bytes=60 * 1024 * 1024
        ),
    )(tiled(states), tiled(stream))
    return ended.transpose(0, 2, 1, 3).reshape(1, BAND, COLS)


def solution(mesh):
    in_specs = (P("cuts", "space", None), P("space", None))
    out_specs = P("cuts", "space", None)
    return jax.shard_map(
        per_device, mesh=mesh, in_specs=in_specs, out_specs=out_specs, check_vma=False
    )
```
